256 devices in a mesh: gx: 64 (over z, x, y_hi), gy: 4 (over y_lo, core).
Axes of the slice: x: 4, y: 4 (y_hi: 2, y_lo: 2; y = y_hi * 2 + y_lo), z: 8, core: 2. Of those that a mesh axis runs over, the one named last changes fastest.
Arguments:
- charges: float32 [1536, 256, 128], P('gx', 'gy'), may hold values from -4 to 4
- kernel_fine: bfloat16 [15, 15, 15], replicated, may hold values from 0 to 1
- kernel_mid: bfloat16 [15, 15, 15], replicated, may hold values from 0 to 1
- kernel_top: bfloat16 [15, 15, 15], replicated, may hold values from 0 to 1
Outputs:
- potential: float32 [1536, 256, 128], P('gx', 'gy')
The draws below stay inside these ranges and needn't reach their ends.
All inputs are finite; a program needn't handle non-finite values.
Results may differ from the reference program's by a relative error of at most 0.0035.
Values may be sent and summed in bfloat16 or wider, within the bound.
A program may use at most 256 MiB of HBM per device.

```python
import jax
import jax.numpy as jnp
from jax import lax

NZ = 128
NX = 1536
NY = 256


def draw_charges(key, part):
    return jnp.clip(jax.random.normal(key, (NX, NY, NZ), jnp.float32), -4.0, 4.0)


def kernel_values(key, level):
    key = jax.random.fold_in(key, 101 + level)
    offsets = jnp.arange(15, dtype=jnp.float32) - 7.0
    radius = offsets[:, None, None] * offsets[:, None, None] + offsets[None, :, None] * offsets[None, :, None] + offsets[None, None, :] * offsets[None, None, :]
    envelope = 1.0 / jnp.sqrt(1.0 + radius / 16.0)
    factor = jax.random.uniform(key, (15, 15, 15), jnp.float32, 0.5, 1.5)
    values = envelope * factor
    values = values * 0.5 ** level / jnp.sqrt(jnp.sum(values * values))
    return values.astype(jnp.bfloat16)


def draw_kernel_fine(key, part):
    return kernel_values(key, 0)


def draw_kernel_mid(key, part):
    return kernel_values(key, 1)


def draw_kernel_top(key, part):
    return kernel_values(key, 2)


def setup_inputs(seed: int = 0) -> dict:
    key_list = jax.random.split(jax.random.key(seed), 5)
    charges = draw_charges(jax.random.fold_in(key_list[4], 71), 0)
    kernel_fine = draw_kernel_fine(jax.random.fold_in(key_list[4], 71), 0)
    kernel_mid = draw_kernel_mid(jax.random.fold_in(key_list[4], 71), 0)
    kernel_top = draw_kernel_top(jax.random.fold_in(key_list[4], 71), 0)
    return dict(charges=charges, kernel_fine=kernel_fine, kernel_mid=kernel_mid, kernel_top=kernel_top)


def restrict_axis(values, axis, count):
    left_part = lax.slice_in_dim(values, 0, 2 * count, 2, axis)
    middle_part = lax.slice_in_dim(values, 1, 2 * count, 2, axis)
    right_part = lax.slice_in_dim(values, 2, 2 * count + 1, 2, axis)
    return 0.5 * left_part + middle_part + 0.5 * right_part


def restrict(field):
    count_x, count_y, count_z = field.shape
    values = jnp.pad(field.astype(jnp.float32), ((1, 0), (1, 0), (1, 0)))
    values = restrict_axis(values, 0, count_x // 2)
    values = restrict_axis(values, 1, count_y // 2)
    return restrict_axis(values, 2, count_z // 2)


def prolong_axis(values, axis, count):
    first_part = lax.slice_in_dim(values, 0, count, 1, axis)
    second_part = lax.slice_in_dim(values, 1, count + 1, 1, axis)
    middle_part = 0.5 * (first_part + second_part)
    joined = jnp.stack((first_part, middle_part), axis=axis + 1)
    new_shape = list(values.shape)
    new_shape[axis] = 2 * count
    return joined.reshape(new_shape)


def prolong(coarse):
    count_x, count_y, count_z = coarse.shape
    values = jnp.pad(coarse, ((0, 1), (0, 1), (0, 1)))
    values = prolong_axis(values, 0, count_x)
    values = prolong_axis(values, 1, count_y)
    return prolong_axis(values, 2, count_z)


def correlate(field, kernel):
    grid_shape = field.shape
    padded_sizes = tuple(extent + 16 for extent in grid_shape)
    flipped = kernel.astype(jnp.float32)[::-1, ::-1, ::-1]
    kernel_grid = jnp.zeros(padded_sizes, field.dtype).at[:15, :15, :15].set(flipped.astype(field.dtype))
    kernel_grid = jnp.roll(kernel_grid, (-7, -7, -7), axis=(0, 1, 2))
    spectrum = jnp.fft.rfftn(field, s=padded_sizes) * jnp.fft.rfftn(kernel_grid, s=padded_sizes)
    result = jnp.fft.irfftn(spectrum, s=padded_sizes)
    return result[:grid_shape[0], :grid_shape[1], :grid_shape[2]].astype(field.dtype)


def widen(values):
    return lax.optimization_barrier(values).astype(jnp.float32)


def reference(charges, kernel_fine, kernel_mid, kernel_top):
    fine_q = charges.astype(jnp.bfloat16)
    mid_r = restrict(widen(fine_q))
    mid_q = mid_r.astype(jnp.bfloat16)
    top_r = restrict(widen(mid_q))
    top_q = top_r.astype(jnp.bfloat16)
    fine_e = correlate(widen(fine_q), kernel_fine)
    mid_e = correlate(widen(mid_q), kernel_mid)
    top_e = correlate(widen(top_q), kernel_top)
    mid_u = mid_e + prolong(top_e)
    return fine_e + prolong(mid_u)
```

```python
import functools

import jax
import jax.numpy as jnp
from jax import lax
from jax.experimental import pallas as pl
from jax.experimental.pallas import tpu as pltpu
from jax.sharding import PartitionSpec as P

MESH = pl.DeviceIdType.MESH
BF, F32 = jnp.bfloat16, jnp.float32

BANDS = ((0, 7, 15), (0, 15, 7), (1, 23, 0), (9, 24, 0), (17, 24, 0))
PAIRS = ((1, 2), (0, 3))
MID_WINDOWS = (0, 2, 1, 3)

ROUND1 = (
    ("x_near", (1, 0)),
    ("y_hi", (0, 1)),
    ("c_hh", (1, 1)),
    ("y_lo", (0, -1)),
    ("x_far", (1, 0)),
    ("x_lo", (-1, 0)),
    ("c_hl", (1, -1)),
    ("c_lh", (-1, 1)),
    ("c_ll", (-1, -1)),
)
MIDS = tuple((dx, dy) for dx in (-1, 0, 1) for dy in (-1, 0, 1) if (dx, dy) != (0, 0))
TOPS = tuple(
    (dx, dy) for dx in (-1, 1, -2, 2, 0) for dy in (0, -1, 1) if (dx, dy) != (0, 0)
)


def iota(shape, dim):
    return lax.broadcasted_iota(jnp.int32, shape, dim)


def dot(a, b):
    return jnp.dot(a, b, preferred_element_type=F32)


def near(twice, other):
    gap = jnp.abs(twice - 2 * other)
    return jnp.where(gap == 0, 1.0, jnp.where(gap == 1, 0.5, 0.0)).astype(F32)


def split(value):
    high = value.astype(BF)
    return high, (value - high.astype(F32)).astype(BF)


def roll(value, shift):
    size = value.shape[-1]
    return value if shift % size == 0 else pltpu.roll(value, shift % size, axis=value.ndim - 1)


def toeplitz_chunks(row):
    block = pltpu.roll(
        jnp.broadcast_to(row, (16, 512)), 1, axis=1, stride=1, stride_axis=0
    )
    block = jnp.concatenate([jnp.zeros((16, 128), F32), block], axis=1)
    return [roll(block, -32 * q).astype(BF) for q in range(4)]


def place(chunks, shift, m):
    q = (-shift) % 4
    n = m + 1 + (-shift - q) // 4
    if 0 <= n <= 4:
        return chunks[q][:, 128 * n : 128 * n + 128]
    return jnp.zeros((16, 128), BF)


def kernel(
    count_x, count_y,
    charges, k_fine, k_mid, k_top, out,
    own, edge, xl, xr, yl, yr, corner,
    mid_pack, mid_edge, mxl, mxr, myl, myr, mid_corner,
    top_pack, top_in,
    taps_in, taps, u_fine, u_mid, u_top, shifted, acc, mid_acc, top_acc,
    rows_mid, rows_top, zx, pxy, pz,
    send_sem, recv_sem,
):
    gx, gy = lax.axis_index("gx"), lax.axis_index("gy")

    def valid(dx, dy):
        ok = jnp.bool_(True)
        if dx:
            ok = (gx + dx >= 0) & (gx + dx < count_x)
        if dy:
            ok = ok & (gy + dy >= 0) & (gy + dy < count_y)
        return ok

    for ref in (xl, xr, yl, yr, corner, mxl, mxr, myl, myr, mid_corner, top_in):
        ref[...] = jnp.zeros_like(ref)
    barrier = pltpu.get_barrier_semaphore()
    for dx, dy in TOPS:

        @pl.when(valid(dx, dy))
        def _(dx=dx, dy=dy):
            pl.semaphore_signal(
                barrier, inc=1, device_id=(gx + dx, gy + dy), device_id_type=MESH
            )

    own[...] = charges[...].astype(BF)
    edge[0] = charges[:, 0:8, :].reshape(12, 16, 128).astype(BF)
    edge[1] = charges[:, 56:64, :].reshape(12, 16, 128).astype(BF)

    taps_in[...] = jnp.zeros_like(taps_in)
    for level, ref in enumerate((k_fine, k_mid, k_top)):
        taps_in[level, :, 0:15, 0:15] = ref[...].astype(F32)
    flat = sum(roll(taps_in[level], 16 * level + 1) for level in range(3))
    flat = flat.reshape(240, 128).astype(BF)
    lane_of = iota((240, 512), 0)
    lane_of = (lane_of // 16) * 32 + lane_of % 16
    spread = jnp.where(lane_of == iota((240, 512), 1), 1.0, 0.0).astype(BF)
    taps[...] = lax.dot_general(
        flat, spread, (((0,), (0,)), ((), ())), preferred_element_type=F32
    )[0:48]

    def fine_weights(step, _):
        chunks = toeplitz_chunks(taps[pl.ds(step, 1), :])
        for r in range(22):
            for m in range(2):
                u_fine[step, 16 * r : 16 * r + 16, 128 * m : 128 * m + 128] = place(
                    chunks, r - 14, m
                )
        return 0

    lax.fori_loop(0, 16, fine_weights, 0)

    messages = {
        "x_near": (own.at[20:24], xl.at[4:8]),
        "x_far": (own.at[17:20], xl.at[1:4]),
        "x_lo": (own.at[0:7], xr.at[0:7]),
        "y_hi": (edge.at[1], yl),
        "y_lo": (edge.at[0], yr),
        "c_hh": (edge.at[1, 8:12], corner.at[0]),
        "c_hl": (edge.at[0, 8:12], corner.at[1]),
        "c_lh": (edge.at[1, 0:4], corner.at[2]),
        "c_ll": (edge.at[0, 0:4], corner.at[3]),
    }
    copies = {}

    def describe(key, source, target, direction):
        dx, dy = direction
        n = len(copies)
        copies[key] = (
            pltpu.make_async_remote_copy(
                src_ref=source,
                dst_ref=target,
                send_sem=send_sem.at[n],
                recv_sem=recv_sem.at[n],
                device_id=(gx + dx, gy + dy),
                device_id_type=MESH,
            ),
            direction,
        )

    def start(key):
        copy, (dx, dy) = copies[key]

        @pl.when(valid(dx, dy))
        def _():
            copy.start()

    def arrived(key):
        copy, (dx, dy) = copies[key]

        @pl.when(valid(-dx, -dy))
        def _():
            copy.wait_recv()

    def sent(key):
        copy, (dx, dy) = copies[key]

        @pl.when(valid(dx, dy))
        def _():
            copy.wait_send()

    for key, direction in ROUND1:
        describe(key, *messages[key], direction)

    in_x = 1 + jnp.minimum(gx, 2) + jnp.minimum(count_x - 1 - gx, 2)
    in_y = 1 + jnp.minimum(gy, 1) + jnp.minimum(count_y - 1 - gy, 1)
    pl.semaphore_wait(barrier, in_x * in_y - 1)
    for key, _ in ROUND1:
        start(key)

    def shift_rows(value, x, y0):
        rows = value.shape[0]
        lane = iota((rows, 128), 1)
        for c in range(4):
            turned = roll(value, -c)
            inside = lane + c < 128
            ahead = jnp.where(inside, turned, 0.0) if c else turned
            behind = jnp.where((lane < 124) | (lane + c >= 128), turned, 0.0)
            shifted[1, c, x, y0 : y0 + rows, :] = ahead.astype(BF)
            shifted[0, c, x, y0 : y0 + rows, :] = behind.astype(BF)

    def fine_products(p, groups):
        def body(s, _):
            side = s // 2
            for k in groups:
                lo, hi, first = BANDS[k]
                rows = 16 * (hi - lo)
                left = jnp.concatenate(
                    [u_fine[4 * s + c, 16 * first : 16 * first + rows, :] for c in range(4)],
                    axis=1,
                )
                right = jnp.concatenate(
                    [
                        jnp.concatenate(
                            [
                                shifted[
                                    side, c, 8 * k : 8 * k + 8, 16 * t : 16 * t + 32, :
                                ].reshape(256, 128)
                                for t in PAIRS[p]
                            ],
                            axis=1,
                        )
                        for c in range(4)
                    ],
                    axis=0,
                )
                acc[s, p, 16 * lo : 16 * hi, :] += dot(left, right)
            return 0

        lax.fori_loop(0, 4, body, 0)

    acc[...] = jnp.zeros_like(acc)

    def inner_rows(x, _):
        shift_rows(charges[x, 8:56, :], x + 8, 16)
        return 0

    lax.fori_loop(0, 24, inner_rows, 0)
    fine_products(0, (1, 2, 3))

    def coarse_weights(step, _):
        chunks = toeplitz_chunks(taps[pl.ds(17 + step, 1), :])
        for i in range(13):
            for m in range(7):
                u_mid[step, 16 * i : 16 * i + 16, 128 * m : 128 * m + 128] = place(
                    chunks, i + 1, m
                )
        chunks = toeplitz_chunks(taps[pl.ds(33 + step, 1), :])
        for i in range(8):
            for m in range(6):
                u_top[step, 16 * i : 16 * i + 16, 128 * m : 128 * m + 128] = place(
                    chunks, i + 1, m
                )
        return 0

    lax.fori_loop(0, 15, coarse_weights, 0)

    r, c = iota((384, 256), 0), iota((384, 256), 1)
    pxy[...] = (near(r // 16, c // 16) * near(r % 16, c % 16)).astype(BF)
    for p in range(2):
        r, c = iota((256, 256), 0), iota((256, 256), 1)
        block = r // 64
        block = jnp.where(block == 1, 2, jnp.where(block == 2, 1, block))
        window = jnp.where(c < 128, PAIRS[p][0], PAIRS[p][1])
        pz[p] = jnp.where(block == window, near(c % 128, r % 64), 0.0).astype(BF)

    for key in ("x_near", "y_hi", "c_hh"):
        arrived(key)
    r, c = iota((128, 128), 0), iota((128, 128), 1)
    halve = near(r, c % 64).astype(BF)
    quarter = jnp.where(r < 64, near(r, c % 32), 0.0).astype(BF)
    side_rows = yl[...].astype(F32).reshape(24, 8, 128)
    body = jnp.concatenate([side_rows, charges[...]], axis=1).reshape(24 * 72, 128)
    zx[4:28] = dot(body.astype(BF), halve).reshape(24, 72, 128)
    side_rows = corner[0].astype(F32).reshape(8, 8, 128)[4:8]
    body = jnp.concatenate([side_rows, xl[4:8].astype(F32)], axis=1).reshape(4 * 72, 128)
    zx[0:4] = dot(body.astype(BF), halve).reshape(4, 72, 128)
    rows_mid[:, 0:16, :] = jnp.zeros((13, 16, 128), F32)
    for i in range(13):
        rows_mid[i, 16:88, :] = (
            0.5 * zx[2 * i + 1] + zx[2 * i + 2] + 0.5 * zx[2 * i + 3]
        )
    mid = (
        0.5 * rows_mid[:, pl.ds(7, 40, 2), :]
        + rows_mid[:, pl.ds(8, 40, 2), :]
        + 0.5 * rows_mid[:, pl.ds(9, 40, 2), :]
    ).astype(BF)
    mid_rows = mid.astype(F32)
    lane = iota((12, 16, 128), 2)
    packed = jnp.where(lane < 64, mid_rows[1:13, 8:24], mid_rows[1:13, 24:40])
    mid_pack[...] = packed.astype(BF)
    mid_edge[0] = packed[:, 0:8].reshape(6, 16, 128).astype(BF)
    mid_edge[1] = packed[:, 8:16].reshape(6, 16, 128).astype(BF)

    mid_messages = {
        (1, 0): (mid_pack.at[5:12], mxl.at[1:8]),
        (-1, 0): (mid_pack.at[0:8], mxr),
        (0, 1): (mid_edge.at[1], myl),
        (0, -1): (mid_edge.at[0], myr),
        (1, 1): (mid_edge.at[1, 2:6], mid_corner.at[0]),
        (1, -1): (mid_edge.at[0, 2:6], mid_corner.at[1]),
        (-1, 1): (mid_edge.at[1, 0:4], mid_corner.at[2]),
        (-1, -1): (mid_edge.at[0, 0:4], mid_corner.at[3]),
    }
    for direction in MIDS:
        describe(("mid", direction), *mid_messages[direction], direction)
        start(("mid", direction))

    zt = dot(mid_rows.reshape(520, 128).astype(BF), quarter).reshape(13, 40, 128)
    for i in range(6):
        rows_top[i] = 0.5 * zt[2 * i] + zt[2 * i + 1] + 0.5 * zt[2 * i + 2]
    top = (
        0.5 * rows_top[:, pl.ds(7, 16, 2), :]
        + rows_top[:, pl.ds(8, 16, 2), :]
        + 0.5 * rows_top[:, pl.ds(9, 16, 2), :]
    )
    lane = iota((6, 8, 128), 2)
    packed = jnp.where(lane % 64 < 32, top[:, 0:8], top[:, 8:16])
    top_pack[...] = packed.reshape(3, 16, 128).astype(BF)
    for direction in TOPS:
        dx, dy = direction
        part = {2: slice(2, 3), -2: slice(0, 1)}.get(dx, slice(0, 3))
        target = top_in.at[2 - dx, 1 - dy, part]
        describe(("top", direction), top_pack.at[part], target, direction)
        start(("top", direction))

    arrived("y_lo")

    def outer_columns(n, _):
        low, high = yl[n].astype(F32), yr[n].astype(F32)
        for h in range(2):
            x = 2 * n + h
            shift_rows(
                jnp.concatenate([low[8 * h : 8 * h + 8], charges[x, 0:8, :]], axis=0),
                x + 8,
                0,
            )
            shift_rows(
                jnp.concatenate([charges[x, 56:64, :], high[8 * h : 8 * h + 8]], axis=0),
                x + 8,
                64,
            )
        return 0

    lax.fori_loop(0, 12, outer_columns, 0)
    fine_products(1, (1, 2, 3))

    for key in ("x_far", "x_lo", "c_hl", "c_lh", "c_ll"):
        arrived(key)

    def outer_rows(n, _):
        for side, rows in ((0, xl), (1, xr)):
            low = corner[2 * side, n].astype(F32)
            high = corner[2 * side + 1, n].astype(F32)
            for h in range(2):
                x = 2 * n + h
                shift_rows(
                    jnp.concatenate(
                        [
                            low[8 * h : 8 * h + 8],
                            rows[x].astype(F32),
                            high[8 * h : 8 * h + 8],
                        ],
                        axis=0,
                    ),
                    x + 32 * side,
                    0,
                )
        return 0

    lax.fori_loop(0, 4, outer_rows, 0)
    fine_products(0, (0, 4))
    fine_products(1, (0, 4))

    for direction in MIDS:
        arrived(("mid", direction))
    centre = jnp.concatenate(
        [mxl[...].astype(F32), mid_pack[...].astype(F32), mxr[...].astype(F32)], axis=0
    )

    def column(first, middle, last):
        return jnp.concatenate(
            [
                first.astype(F32).reshape(8, 8, 128),
                middle.astype(F32).reshape(12, 8, 128),
                last.astype(F32).reshape(8, 8, 128),
            ],
            axis=0,
        )

    low = column(mid_corner[0], myl[...], mid_corner[2])
    high = column(mid_corner[1], myr[...], mid_corner[3])
    lane = iota((28, 8, 128), 2)
    low = roll(jnp.where(lane < 64, centre[:, 8:16], low), 64)
    high = roll(jnp.where(lane < 64, high, centre[:, 0:8]), 64)
    field = jnp.concatenate([low, centre, high], axis=1).reshape(896, 128).astype(BF)

    for direction in TOPS:
        arrived(("top", direction))

    def strip(dy):
        parts = []
        for dx in (-2, -1, 0, 1, 2):
            if dx == 0 and dy == 0:
                value = top_pack[...]
            elif dx == -2:
                value = top_in[0, 1 + dy, 2:3]
            elif dx == 2:
                value = top_in[4, 1 + dy, 0:1]
            else:
                value = top_in[2 + dx, 1 + dy]
            parts.append(value.astype(F32).reshape(2 * value.shape[0], 8, 128))
        return jnp.concatenate(parts, axis=0)

    centre, low, high = strip(0), strip(-1), strip(1)
    lane = iota((22, 8, 128), 2) % 64
    low = roll(jnp.where(lane < 32, centre, low), 32)
    high = roll(jnp.where(lane < 32, high, centre), 32)
    top_field = jnp.concatenate([low, centre, high], axis=1).reshape(528, 128).astype(BF)

    mid_acc[...] = jnp.zeros_like(mid_acc)
    top_acc[...] = jnp.zeros_like(top_acc)
    r, c = iota((128, 128), 0), iota((128, 128), 1)

    def coarse_products(step, _):
        hit = r == c + (step - 7)
        move = jnp.where(hit & (r // 64 == c // 64), 1.0, 0.0).astype(BF)
        moved = dot(field, move).reshape(28, 32, 128)
        right = jnp.concatenate(
            [
                moved,
                jnp.concatenate([moved[:, 8:32], moved[:, 0:8]], axis=1),
            ],
            axis=2,
        )
        mid_acc[0:208] += dot(u_mid[step], right.reshape(896, 256).astype(BF))
        move = jnp.where(hit & (r // 32 == c // 32), 1.0, 0.0).astype(BF)
        moved = dot(top_field, move).reshape(22, 24, 128)
        right = jnp.concatenate([moved, jnp.zeros((22, 8, 128), F32)], axis=1)
        right = jnp.concatenate([right.reshape(704, 128), jnp.zeros((64, 128), F32)], axis=0)
        top_acc[...] += dot(u_top[step], right.astype(BF))
        return 0

    lax.fori_loop(0, 15, coarse_products, 0)

    last_x, last_y = gx == count_x - 1, gy == count_y - 1
    r, c = iota((128, 128), 0), iota((128, 128), 1)
    beyond = (last_x & (r // 16 == 6)) | (last_y & (r % 16 == 8) & (c % 64 >= 32))
    high, low = split(jnp.where(beyond, 0.0, top_acc[...]))
    stretch = jnp.where(
        (r < 64) & (r // 32 == c // 64), near(c % 64, r % 32), 0.0
    ).astype(BF)
    wide = dot(
        jnp.concatenate([high, low], axis=1), jnp.concatenate([stretch, stretch], axis=0)
    )
    wide = jnp.concatenate(split(wide), axis=0)
    r, c = iota((208, 128), 0), iota((208, 128), 1)
    along_x = near(r // 16, c // 16)
    parts = []
    for parity in range(2):
        weights = (along_x * near(8 * parity + r % 16, c % 16)).astype(BF)
        parts.append(dot(jnp.concatenate([weights, weights], axis=1), wide))
    mid_u = mid_acc[0:208] + jnp.concatenate(parts, axis=1)

    r, c = iota((208, 256), 0), iota((208, 256), 1)
    beyond = (last_x & (r // 16 == 12)) | (last_y & (r % 16 == 8) & (c >= 192))
    mid_u = jnp.concatenate(split(jnp.where(beyond, 0.0, mid_u)), axis=1)
    weights = jnp.concatenate([pxy[...], pxy[...]], axis=1)
    lane = iota((384, 128), 1)
    for p in range(2):
        wide = dot(mid_u, jnp.concatenate([pz[p], pz[p]], axis=0))
        high, low = split(jnp.concatenate([wide, jnp.zeros((48, 256), F32)], axis=0))
        total = dot(weights, jnp.concatenate([high, low], axis=0))
        for h in range(2):
            lanes = slice(128 * h, 128 * h + 128)
            value = total[:, lanes] + acc[2, p, :, lanes]
            value += jnp.where(lane < 124, roll(acc[3, p, :, lanes], -4), 0.0)
            value += roll(acc[1, p, :, lanes], 4)
            value += jnp.where(lane >= 4, roll(acc[0, p, :, lanes], 8), 0.0)
            t = PAIRS[p][h]
            out[:, 16 * t : 16 * t + 16, :] = value.reshape(24, 16, 128)

    for key in copies:
        sent(key)


def solution(mesh):
    count_x, count_y = mesh.shape["gx"], mesh.shape["gy"]
    vmem = pl.BlockSpec(memory_space=pltpu.VMEM)
    messages = len(ROUND1) + len(MIDS) + len(TOPS)

    def shards(charges, kernel_fine, kernel_mid, kernel_top):
        return pl.pallas_call(
            functools.partial(kernel, count_x, count_y),
            out_shape=jax.ShapeDtypeStruct(charges.shape, F32),
            in_specs=[vmem] * 4,
            out_specs=vmem,
            scratch_shapes=[
                pltpu.VMEM((24, 64, 128), BF),
                pltpu.VMEM((2, 12, 16, 128), BF),
                pltpu.VMEM((8, 64, 128), BF),
                pltpu.VMEM((8, 64, 128), BF),
                pltpu.VMEM((12, 16, 128), BF),
                pltpu.VMEM((12, 16, 128), BF),
                pltpu.VMEM((4, 4, 16, 128), BF),
                pltpu.VMEM((12, 16, 128), BF),
                pltpu.VMEM((2, 6, 16, 128), BF),
                pltpu.VMEM((8, 16, 128), BF),
                pltpu.VMEM((8, 16, 128), BF),
                pltpu.VMEM((6, 16, 128), BF),
                pltpu.VMEM((6, 16, 128), BF),
                pltpu.VMEM((4, 4, 16, 128), BF),
                pltpu.VMEM((3, 16, 128), BF),
                pltpu.VMEM((5, 3, 3, 16, 128), BF),
                pltpu.VMEM((3, 15, 16, 128), F32),
                pltpu.VMEM((48, 512), F32),
                pltpu.VMEM((16, 352, 256), BF),
                pltpu.VMEM((15, 208, 896), BF),
                pltpu.VMEM((15, 128, 768), BF),
                pltpu.VMEM((2, 4, 40, 80, 128), BF),
                pltpu.VMEM((4, 2, 384, 256), F32),
                pltpu.VMEM((208, 256), F32),
                pltpu.VMEM((128, 128), F32),
                pltpu.VMEM((13, 88, 128), F32),
                pltpu.VMEM((6, 40, 128), F32),
                pltpu.VMEM((28, 72, 128), F32),
                pltpu.VMEM((384, 256), BF),
                pltpu.VMEM((2, 256, 256), BF),
                pltpu.SemaphoreType.DMA((messages,)),
                pltpu.SemaphoreType.DMA((messages,)),
            ],
            compiler_params=pltpu.CompilerParams(
                collective_id=0, has_side_effects=True, vmem_limit_bytes=56 * 2**20
            ),
        )(charges, kernel_fine, kernel_mid, kernel_top)

    placed = (P("gx", "gy", None), P(), P(), P())
    return jax.shard_map(
        shards, mesh=mesh, in_specs=placed, out_specs=P("gx", "gy", None), check_vma=False
    )
```

```python
import functools

import jax
import jax.numpy as jnp
from jax import lax
from jax.experimental import pallas as pl
from jax.experimental.pallas import tpu as pltpu
from jax.sharding import PartitionSpec as P

MESH = pl.DeviceIdType.MESH
BF, F32 = jnp.bfloat16, jnp.float32

BANDS = ((0, 7, 15), (0, 15, 7), (1, 23, 0), (9, 24, 0), (17, 24, 0))
PAIRS = ((1, 2), (0, 3))
MID_WINDOWS = (0, 2, 1, 3)

ROUND1 = (
    ("x_near", (1, 0)),
    ("y_hi", (0, 1)),
    ("c_hh", (1, 1)),
    ("y_lo", (0, -1)),
    ("x_far", (1, 0)),
    ("x_lo", (-1, 0)),
    ("c_hl", (1, -1)),
    ("c_lh", (-1, 1)),
    ("c_ll", (-1, -1)),
)
MIDS = tuple((dx, dy) for dx in (-1, 0, 1) for dy in (-1, 0, 1) if (dx, dy) != (0, 0))
TOPS = tuple(
    (dx, dy) for dx in (-1, 1, -2, 2, 0) for dy in (0, -1, 1) if (dx, dy) != (0, 0)
)


def iota(shape, dim):
    return lax.broadcasted_iota(jnp.int32, shape, dim)


def dot(a, b):
    return jnp.dot(a, b, preferred_element_type=F32)


def near(twice, other):
    gap = jnp.abs(twice - 2 * other)
    return jnp.where(gap == 0, 1.0, jnp.where(gap == 1, 0.5, 0.0)).astype(F32)


def split(value):
    high = value.astype(BF)
    return high, (value - high.astype(F32)).astype(BF)


def roll(value, shift):
    size = value.shape[-1]
    return value if shift % size == 0 else pltpu.roll(value, shift % size, axis=value.ndim - 1)


def toeplitz_chunks(row):
    block = pltpu.roll(
        jnp.broadcast_to(row, (16, 512)), 1, axis=1, stride=1, stride_axis=0
    )
    block = jnp.concatenate([jnp.zeros((16, 128), F32), block], axis=1)
    return jnp.concatenate([roll(block, -32 * q).astype(BF) for q in range(4)], axis=1)


def place(chunks, index, shift, m):
    q = (-shift) % 4
    n = m + 1 + (-shift - q) // 4
    if 0 <= n <= 4:
        return chunks[index, :, 640 * q + 128 * n : 640 * q + 128 * n + 128]
    return jnp.zeros((16, 128), BF)


def weights(chunks, indices, shifts, lanes):
    return jnp.concatenate(
        [
            jnp.concatenate(
                [place(chunks, i, shift, m) for i in indices for m in range(lanes // 128)],
                axis=1,
            )
            for shift in shifts
        ],
        axis=0,
    )


def moves(c, size):
    r, l = iota((128, 128), 0), iota((128, 128), 1)
    at = l % size
    ahead = (r == l + c) & (at + c < size)
    behind = ((r == l + c) & (at < size - 4)) | ((r == l + c - size) & (at + c >= size))
    return jnp.concatenate(
        [jnp.where(behind, 1.0, 0.0), jnp.where(ahead, 1.0, 0.0)], axis=1
    ).astype(BF)


def gather(parts, size):
    at = iota(parts[0].shape, 1) % size
    value = parts[2] + jnp.where(at < size - 4, roll(parts[3], -4), 0.0)
    value += jnp.where(at >= 4, roll(parts[1], 4), roll(parts[1], 4 - size))
    back = jnp.where(at >= 4, roll(parts[0], 8 - size), 0.0)
    return value + jnp.where(at >= 8, roll(parts[0], 8), back)


def kernel(
    count_x, count_y,
    charges_in, k_fine, k_mid, k_top, out,
    charges, own, edge, xl, xr, yl, yr, corner,
    mid_pack, mid_edge, mxl, mxr, myl, myr, mid_corner,
    top_pack, top_in,
    taps_in, taps, chunks, inner, outer, acc, mid_acc, top_acc, mid_right, top_right,
    rows_mid, rows_top, zx, pxy, pz,
    load_sem, send_sem, recv_sem,
):
    gx, gy = lax.axis_index("gx"), lax.axis_index("gy")

    def valid(dx, dy):
        ok = jnp.bool_(True)
        if dx:
            ok = (gx + dx >= 0) & (gx + dx < count_x)
        if dy:
            ok = ok & (gy + dy >= 0) & (gy + dy < count_y)
        return ok

    load = pltpu.make_async_copy(charges_in, charges, load_sem)
    load.start()

    @pl.when((gx < 2) | (gx >= count_x - 2) | (gy == 0) | (gy == count_y - 1))
    def _():
        for ref in (yl, yr, corner, mxl, mxr, myl, myr, mid_corner, top_in):
            ref[...] = jnp.zeros_like(ref)

    for ref, dx in ((xl, -1), (xr, 1)):

        @pl.when(~valid(dx, 0))
        def _(ref=ref):
            ref[...] = jnp.zeros_like(ref)

    for ref in (xl.at[0], xr.at[7], mxl.at[0]):
        ref[...] = jnp.zeros(ref.shape, BF)
    barrier = pltpu.get_barrier_semaphore()
    for dx, dy in TOPS:

        @pl.when(valid(dx, dy))
        def _(dx=dx, dy=dy):
            pl.semaphore_signal(
                barrier, inc=1, device_id=(gx + dx, gy + dy), device_id_type=MESH
            )

    taps_in[...] = jnp.zeros_like(taps_in)
    for level, ref in enumerate((k_fine, k_mid, k_top)):
        taps_in[level, :, 0:15, 0:15] = ref[...].astype(F32)
    flat = sum(roll(taps_in[level], 16 * level + 1) for level in range(3))
    flat = flat.reshape(240, 128).astype(BF)
    lane_of = iota((240, 512), 0)
    lane_of = (lane_of // 16) * 32 + lane_of % 16
    spread = jnp.where(lane_of == iota((240, 512), 1), 1.0, 0.0).astype(BF)
    taps[...] = lax.dot_general(
        flat, spread, (((0,), (0,)), ((), ())), preferred_element_type=F32
    )[0:48]

    load.wait()
    own[...] = charges[...].astype(BF)
    edge[0] = charges[:, 0:8, :].reshape(12, 16, 128).astype(BF)
    edge[1] = charges[:, 56:64, :].reshape(12, 16, 128).astype(BF)

    def build(row):
        chunks[row] = toeplitz_chunks(taps[pl.ds(row, 1), :])

    messages = {
        "x_near": (own.at[20:24], xl.at[4:8]),
        "x_far": (own.at[17:20], xl.at[1:4]),
        "x_lo": (own.at[0:7], xr.at[0:7]),
        "y_hi": (edge.at[1], yl),
        "y_lo": (edge.at[0], yr),
        "c_hh": (edge.at[1, 8:12], corner.at[0]),
        "c_hl": (edge.at[0, 8:12], corner.at[1]),
        "c_lh": (edge.at[1, 0:4], corner.at[2]),
        "c_ll": (edge.at[0, 0:4], corner.at[3]),
    }
    copies = {}

    def describe(key, source, target, direction):
        dx, dy = direction
        n = len(copies)
        copies[key] = (
            pltpu.make_async_remote_copy(
                src_ref=source,
                dst_ref=target,
                send_sem=send_sem.at[n],
                recv_sem=recv_sem.at[n],
                device_id=(gx + dx, gy + dy),
                device_id_type=MESH,
            ),
            direction,
        )

    def start(key):
        copy, (dx, dy) = copies[key]

        @pl.when(valid(dx, dy))
        def _():
            copy.start()

    def arrived(key):
        copy, (dx, dy) = copies[key]

        @pl.when(valid(-dx, -dy))
        def _():
            copy.wait_recv()

    def sent(key):
        copy, (dx, dy) = copies[key]

        @pl.when(valid(dx, dy))
        def _():
            copy.wait_send()

    for key, direction in ROUND1:
        describe(key, *messages[key], direction)

    def shift_rows(value, x, target):
        rows = value.shape[0]
        lane = iota((rows, 128), 1)
        for c in range(4):
            turned = roll(value, -c)
            ahead = jnp.where(lane + c < 128, turned, 0.0) if c else turned
            behind = jnp.where((lane < 124) | (lane + c >= 128), turned, 0.0)
            target[1, c, x] = ahead.astype(BF)
            target[0, c, x] = behind.astype(BF)

    def window(side, c, k, t):
        group = pl.ds(8 * k, 8)
        if t == 0:
            parts = [outer[0, side, c, group], inner[side, c, group, 0:16, :]]
        elif t == 3:
            parts = [inner[side, c, group, 32:48, :], outer[1, side, c, group]]
        else:
            parts = [inner[side, c, group, 16 * t - 16 : 16 * t + 16, :]]
        return jnp.concatenate(parts, axis=1).reshape(256, 128)

    def fine_product(s, p, k):
        lo, hi, first = BANDS[k]
        left = weights(
            chunks, [4 * s + c for c in range(4)], range(first - 14, first - 14 + hi - lo), 256
        )
        right = jnp.concatenate(
            [
                jnp.concatenate([window(s // 2, c, k, t) for t in PAIRS[p]], axis=1)
                for c in range(4)
            ],
            axis=0,
        )
        return dot(left, right)

    def fine_centre(s, p):
        one, two, three = (fine_product(s, p, k) for k in (1, 2, 3))
        acc[s, p, 0:16] = one[0:16]
        acc[s, p, 16:144] = one[16:144] + two[0:128]
        acc[s, p, 144:240] = one[144:240] + two[128:224] + three[0:96]
        acc[s, p, 240:368] = two[224:352] + three[96:224]
        acc[s, p, 368:384] = three[224:240]

    def first_steps(n, _):
        for h in range(2):
            build(2 * n + h)
        for h in range(3):
            x = 3 * n + h
            shift_rows(charges[x, 8:56, :], x + 8, inner)
        return 0

    lax.fori_loop(0, 8, first_steps, 0)

    in_x = 1 + jnp.minimum(gx, 2) + jnp.minimum(count_x - 1 - gx, 2)
    in_y = 1 + jnp.minimum(gy, 1) + jnp.minimum(count_y - 1 - gy, 1)
    pl.semaphore_wait(barrier, in_x * in_y - 1)
    for key, _ in ROUND1:
        start(key)

    def second_steps(s, _):
        fine_centre(s, 0)
        for h in range(8):
            build(16 + 8 * s + h)
        return 0

    lax.fori_loop(0, 4, second_steps, 0)

    r, c = iota((384, 256), 0), iota((384, 256), 1)
    pxy[...] = (near(r // 16, c // 16) * near(r % 16, c % 16)).astype(BF)
    for p in range(2):
        r, c = iota((256, 256), 0), iota((256, 256), 1)
        block = r // 64
        block = jnp.where(block == 1, 2, jnp.where(block == 2, 1, block))
        column_of = jnp.where(c < 128, PAIRS[p][0], PAIRS[p][1])
        pz[p] = jnp.where(block == column_of, near(c % 128, r % 64), 0.0).astype(BF)

    for key in ("x_near", "y_hi", "c_hh"):
        arrived(key)
    r, c = iota((128, 128), 0), iota((128, 128), 1)
    halve = near(r, c % 64).astype(BF)
    quarter = jnp.where(r < 64, near(r, c % 32), 0.0).astype(BF)
    side_rows = yl[...].astype(F32).reshape(24, 8, 128)
    body = jnp.concatenate([side_rows, charges[...]], axis=1).reshape(24 * 72, 128)
    zx[4:28] = dot(body.astype(BF), halve).reshape(24, 72, 128)
    side_rows = corner[0].astype(F32).reshape(8, 8, 128)[4:8]
    body = jnp.concatenate([side_rows, xl[4:8].astype(F32)], axis=1).reshape(4 * 72, 128)
    zx[0:4] = dot(body.astype(BF), halve).reshape(4, 72, 128)
    rows_mid[:, 0:16, :] = jnp.zeros((13, 16, 128), F32)
    for i in range(13):
        rows_mid[i, 16:88, :] = (
            0.5 * zx[2 * i + 1] + zx[2 * i + 2] + 0.5 * zx[2 * i + 3]
        )
    mid = (
        0.5 * rows_mid[:, pl.ds(7, 40, 2), :]
        + rows_mid[:, pl.ds(8, 40, 2), :]
        + 0.5 * rows_mid[:, pl.ds(9, 40, 2), :]
    ).astype(BF)
    mid_rows = mid.astype(F32)
    lane = iota((12, 16, 128), 2)
    packed = jnp.where(lane < 64, mid_rows[1:13, 8:24], mid_rows[1:13, 24:40])
    mid_pack[...] = packed.astype(BF)
    mid_edge[0] = packed[:, 0:8].reshape(6, 16, 128).astype(BF)
    mid_edge[1] = packed[:, 8:16].reshape(6, 16, 128).astype(BF)

    mid_messages = {
        (1, 0): (mid_pack.at[5:12], mxl.at[1:8]),
        (-1, 0): (mid_pack.at[0:8], mxr),
        (0, 1): (mid_edge.at[1], myl),
        (0, -1): (mid_edge.at[0], myr),
        (1, 1): (mid_edge.at[1, 2:6], mid_corner.at[0]),
        (1, -1): (mid_edge.at[0, 2:6], mid_corner.at[1]),
        (-1, 1): (mid_edge.at[1, 0:4], mid_corner.at[2]),
        (-1, -1): (mid_edge.at[0, 0:4], mid_corner.at[3]),
    }
    for direction in MIDS:
        describe(("mid", direction), *mid_messages[direction], direction)
        start(("mid", direction))

    zt = dot(mid_rows.reshape(520, 128).astype(BF), quarter).reshape(13, 40, 128)
    for i in range(6):
        rows_top[i] = 0.5 * zt[2 * i] + zt[2 * i + 1] + 0.5 * zt[2 * i + 2]
    top = (
        0.5 * rows_top[:, pl.ds(7, 16, 2), :]
        + rows_top[:, pl.ds(8, 16, 2), :]
        + 0.5 * rows_top[:, pl.ds(9, 16, 2), :]
    )
    lane = iota((6, 8, 128), 2)
    packed = jnp.where(lane % 64 < 32, top[:, 0:8], top[:, 8:16])
    top_pack[...] = packed.reshape(3, 16, 128).astype(BF)
    for direction in TOPS:
        dx, dy = direction
        part = {2: slice(2, 3), -2: slice(0, 1)}.get(dx, slice(0, 3))
        target = top_in.at[2 - dx, 1 - dy, part]
        describe(("top", direction), top_pack.at[part], target, direction)
        start(("top", direction))

    arrived("y_lo")

    def outer_columns(n, _):
        low, high = yl[n].astype(F32), yr[n].astype(F32)
        for h in range(2):
            x = 2 * n + h
            shift_rows(
                jnp.concatenate([low[8 * h : 8 * h + 8], charges[x, 0:8, :]], axis=0),
                x + 8,
                outer.at[0],
            )
            shift_rows(
                jnp.concatenate([charges[x, 56:64, :], high[8 * h : 8 * h + 8]], axis=0),
                x + 8,
                outer.at[1],
            )
        return 0

    lax.fori_loop(0, 12, outer_columns, 0, unroll=2)

    def third_steps(s, _):
        fine_centre(s, 1)
        return 0

    lax.fori_loop(0, 4, third_steps, 0)

    for key in ("x_far", "x_lo", "c_hl", "c_lh", "c_ll"):
        arrived(key)

    def outer_rows(n, _):
        for side, rows in ((0, xl), (1, xr)):
            low = corner[2 * side, n].astype(F32)
            high = corner[2 * side + 1, n].astype(F32)
            for h in range(2):
                x = 2 * n + h
                target = x + 32 * side
                row = rows[x].astype(F32)
                part = slice(8 * h, 8 * h + 8)
                shift_rows(row[8:56], target, inner)
                shift_rows(jnp.concatenate([low[part], row[0:8]], axis=0), target, outer.at[0])
                shift_rows(jnp.concatenate([row[56:64], high[part]], axis=0), target, outer.at[1])
        return 0

    lax.fori_loop(0, 4, outer_rows, 0)

    def fourth_steps(s, _):
        for p in range(2):
            for k in (0, 4):
                lo, hi, _ = BANDS[k]
                acc[s, p, 16 * lo : 16 * hi, :] += fine_product(s, p, k)
        return 0

    lax.fori_loop(0, 4, fourth_steps, 0)

    def mid_field(centre, low, high):
        lane = iota(low.shape, 2)
        first = roll(jnp.where(lane < 64, centre[:, 8:16], low), 64)
        last = roll(jnp.where(lane < 64, high, centre[:, 0:8]), 64)
        field = jnp.concatenate([first, centre, last], axis=1)
        return field.reshape(32 * field.shape[0], 128).astype(BF)

    def mid_shift(field, start):
        rows = field.shape[0]
        for c in range(4):
            moved = dot(field, moves(c, 64)).reshape(rows // 32, 32, 256)
            turned = jnp.concatenate([moved[:, 8:32], moved[:, 0:8]], axis=1)
            for side in range(2):
                lanes = slice(128 * side, 128 * side + 128)
                both = jnp.concatenate([moved[:, :, lanes], turned[:, :, lanes]], axis=2)
                mid_right[side, c, start : start + rows, :] = both.reshape(rows, 256).astype(BF)

    def mid_product(s, blocks, start, rows):
        left = weights(
            chunks,
            [16 + 4 * s + c for c in range(4)],
            [i + 1 - start // 32 for i in blocks],
            rows,
        )
        right = jnp.concatenate(
            [mid_right[s // 2, c, start : start + rows, :] for c in range(4)], axis=0
        )
        return dot(left, right)

    def pairs(ref):
        value = ref[...].astype(F32)
        return value.reshape(2 * value.shape[0], 8, 128)

    for direction in ((0, 1), (0, -1)):
        arrived(("mid", direction))
    mid_shift(mid_field(mid_pack[...].astype(F32), pairs(myl), pairs(myr)), 256)

    def fifth_steps(s, _):
        mid_acc[s] = mid_product(s, range(13), 256, 384)
        return 0

    lax.fori_loop(0, 4, fifth_steps, 0)

    for direction in MIDS:
        if direction[0]:
            arrived(("mid", direction))
    for side, rows in ((0, mxl), (1, mxr)):
        low, high = pairs(mid_corner.at[2 * side]), pairs(mid_corner.at[2 * side + 1])
        mid_shift(mid_field(rows[...].astype(F32), low, high), 640 * side)

    for direction in TOPS:
        arrived(("top", direction))

    def strip(dy):
        parts = []
        for dx in (-2, -1, 0, 1, 2):
            if dx == 0 and dy == 0:
                ref = top_pack
            elif dx == -2:
                ref = top_in.at[0, 1 + dy, 2:3]
            elif dx == 2:
                ref = top_in.at[4, 1 + dy, 0:1]
            else:
                ref = top_in.at[2 + dx, 1 + dy]
            parts.append(pairs(ref))
        return jnp.concatenate(parts, axis=0)

    centre, low, high = strip(0), strip(-1), strip(1)
    lane = iota((22, 8, 128), 2) % 64
    low = roll(jnp.where(lane < 32, centre, low), 32)
    high = roll(jnp.where(lane < 32, high, centre), 32)
    field = jnp.concatenate([low, centre, high], axis=1).reshape(528, 128).astype(BF)
    lane = iota((20, 24, 128), 2)
    for c in range(4):
        moved = dot(field, moves(c, 32)).reshape(22, 24, 256)
        moved = jnp.concatenate([moved, jnp.zeros((2, 24, 256), F32)], axis=0)
        for side in range(2):
            part = moved[:, :, 128 * side : 128 * side + 128]
            both = jnp.where(lane < 64, part[0:20], part[4:24])
            both = jnp.concatenate([both, jnp.zeros((20, 8, 128), F32)], axis=1)
            top_right[side, c] = both.reshape(640, 128).astype(BF)

    def sixth_steps(s, _):
        mid_acc[s, 0:112, :] += mid_product(s, range(7), 0, 256)
        mid_acc[s, 80:208, :] += mid_product(s, range(5, 13), 640, 256)
        left = weights(chunks, [32 + 4 * s + c for c in range(4)], range(1, 5), 640)
        right = jnp.concatenate([top_right[s // 2, c] for c in range(4)], axis=0)
        top_acc[s] = dot(left, right)
        return 0

    lax.fori_loop(0, 4, sixth_steps, 0)

    last_x, last_y = gx == count_x - 1, gy == count_y - 1
    r, c = iota((128, 128), 0), iota((128, 128), 1)
    beyond = (last_x & (r // 16 == 6)) | (last_y & (r % 16 == 8) & (c % 64 >= 32))
    top_e = gather([top_acc[s] for s in range(4)], 32)
    top_e = jnp.concatenate([top_e, roll(top_e, 64)], axis=0)
    high, low = split(jnp.where(beyond, 0.0, top_e))
    stretch = jnp.where(
        (r < 64) & (r // 32 == c // 64), near(c % 64, r % 32), 0.0
    ).astype(BF)
    wide = dot(
        jnp.concatenate([high, low], axis=1), jnp.concatenate([stretch, stretch], axis=0)
    )
    wide = jnp.concatenate(split(wide), axis=0)
    r, c = iota((208, 128), 0), iota((208, 128), 1)
    along_x = near(r // 16, c // 16)
    parts = []
    for parity in range(2):
        spread = (along_x * near(8 * parity + r % 16, c % 16)).astype(BF)
        parts.append(dot(jnp.concatenate([spread, spread], axis=1), wide))
    mid_u = gather([mid_acc[s] for s in range(4)], 64) + jnp.concatenate(parts, axis=1)

    r, c = iota((208, 256), 0), iota((208, 256), 1)
    beyond = (last_x & (r // 16 == 12)) | (last_y & (r % 16 == 8) & (c >= 192))
    mid_u = jnp.concatenate(split(jnp.where(beyond, 0.0, mid_u)), axis=1)
    spread = jnp.concatenate([pxy[...], pxy[...]], axis=1)
    lane = iota((384, 128), 1)
    for p in range(2):
        wide = dot(mid_u, jnp.concatenate([pz[p], pz[p]], axis=0))
        high, low = split(jnp.concatenate([wide, jnp.zeros((48, 256), F32)], axis=0))
        total = dot(spread, jnp.concatenate([high, low], axis=0))
        for h in range(2):
            lanes = slice(128 * h, 128 * h + 128)
            value = total[:, lanes] + acc[2, p, :, lanes]
            value += jnp.where(lane < 124, roll(acc[3, p, :, lanes], -4), 0.0)
            value += roll(acc[1, p, :, lanes], 4)
            value += jnp.where(lane >= 4, roll(acc[0, p, :, lanes], 8), 0.0)
            t = PAIRS[p][h]
            out[:, 16 * t : 16 * t + 16, :] = value.reshape(24, 16, 128)

    for key in copies:
        sent(key)


def solution(mesh):
    count_x, count_y = mesh.shape["gx"], mesh.shape["gy"]
    vmem = pl.BlockSpec(memory_space=pltpu.VMEM)
    messages = len(ROUND1) + len(MIDS) + len(TOPS)

    def shards(charges, kernel_fine, kernel_mid, kernel_top):
        return pl.pallas_call(
            functools.partial(kernel, count_x, count_y),
            out_shape=jax.ShapeDtypeStruct(charges.shape, F32),
            in_specs=[pl.BlockSpec(memory_space=pl.ANY)] + [vmem] * 3,
            out_specs=vmem,
            scratch_shapes=[
                pltpu.VMEM((24, 64, 128), F32),
                pltpu.VMEM((24, 64, 128), BF),
                pltpu.VMEM((2, 12, 16, 128), BF),
                pltpu.VMEM((8, 64, 128), BF),
                pltpu.VMEM((8, 64, 128), BF),
                pltpu.VMEM((12, 16, 128), BF),
                pltpu.VMEM((12, 16, 128), BF),
                pltpu.VMEM((4, 4, 16, 128), BF),
                pltpu.VMEM((12, 16, 128), BF),
                pltpu.VMEM((2, 6, 16, 128), BF),
                pltpu.VMEM((8, 16, 128), BF),
                pltpu.VMEM((8, 16, 128), BF),
                pltpu.VMEM((6, 16, 128), BF),
                pltpu.VMEM((6, 16, 128), BF),
                pltpu.VMEM((4, 4, 16, 128), BF),
                pltpu.VMEM((3, 16, 128), BF),
                pltpu.VMEM((5, 3, 3, 16, 128), BF),
                pltpu.VMEM((3, 15, 16, 128), F32),
                pltpu.VMEM((48, 512), F32),
                pltpu.VMEM((48, 16, 2560), BF),
                pltpu.VMEM((2, 4, 40, 48, 128), BF),
                pltpu.VMEM((2, 2, 4, 40, 16, 128), BF),
                pltpu.VMEM((4, 2, 384, 256), F32),
                pltpu.VMEM((4, 208, 256), F32),
                pltpu.VMEM((4, 64, 128), F32),
                pltpu.VMEM((2, 4, 896, 256), BF),
                pltpu.VMEM((2, 4, 640, 128), BF),
                pltpu.VMEM((13, 88, 128), F32),
                pltpu.VMEM((6, 40, 128), F32),
                pltpu.VMEM((28, 72, 128), F32),
                pltpu.VMEM((384, 256), BF),
                pltpu.VMEM((2, 256, 256), BF),
                pltpu.SemaphoreType.DMA,
                pltpu.SemaphoreType.DMA((messages,)),
                pltpu.SemaphoreType.DMA((messages,)),
            ],
            compiler_params=pltpu.CompilerParams(
                collective_id=0, has_side_effects=True, vmem_limit_bytes=56 * 2**20
            ),
        )(charges, kernel_fine, kernel_mid, kernel_top)

    placed = (P("gx", "gy", None), P(), P(), P())
    return jax.shard_map(
        shards, mesh=mesh, in_specs=placed, out_specs=P("gx", "gy", None), check_vma=False
    )
```

```python
import functools

import jax
import jax.numpy as jnp
from jax import lax
from jax.experimental import pallas as pl
from jax.experimental.pallas import tpu as pltpu
from jax.sharding import PartitionSpec as P

MESH = pl.DeviceIdType.MESH
BF, F32 = jnp.bfloat16, jnp.float32

BANDS = ((0, 7, 15), (0, 15, 7), (1, 23, 0), (9, 24, 0), (17, 24, 0))
PAIRS = ((1, 2), (0, 3))
MID_WINDOWS = (0, 2, 1, 3)

ROUND1 = (
    ("x_near", (1, 0)),
    ("y_hi", (0, 1)),
    ("c_hh", (1, 1)),
    ("y_lo", (0, -1)),
    ("x_far", (1, 0)),
    ("x_lo", (-1, 0)),
    ("c_hl", (1, -1)),
    ("c_lh", (-1, 1)),
    ("c_ll", (-1, -1)),
)
EARLY = ("x_near", "y_hi", "c_hh", "y_lo", "x_far", "x_lo", "c_hl", "c_lh", "c_ll")
LATE = ()
MIDS = tuple((dx, dy) for dx in (-1, 0, 1) for dy in (-1, 0, 1) if (dx, dy) != (0, 0))
TOPS = tuple(
    (dx, dy) for dx in (-1, 1, -2, 2, 0) for dy in (0, -1, 1) if (dx, dy) != (0, 0)
)


def iota(shape, dim):
    return lax.broadcasted_iota(jnp.int32, shape, dim)


def dot(a, b):
    return jnp.dot(a, b, preferred_element_type=F32)


def near(twice, other):
    gap = jnp.abs(twice - 2 * other)
    return jnp.where(gap == 0, 1.0, jnp.where(gap == 1, 0.5, 0.0)).astype(F32)


def split(value):
    high = value.astype(BF)
    return high, (value - high.astype(F32)).astype(BF)


def roll(value, shift):
    size = value.shape[-1]
    return value if shift % size == 0 else pltpu.roll(value, shift % size, axis=value.ndim - 1)


def toeplitz_chunks(row):
    block = pltpu.roll(
        jnp.broadcast_to(row, (16, 512)), 1, axis=1, stride=1, stride_axis=0
    )
    block = jnp.concatenate([jnp.zeros((16, 128), F32), block], axis=1)
    return jnp.concatenate([roll(block, -32 * q).astype(BF) for q in range(4)], axis=1)


def place(chunks, index, shift, m):
    q = (-shift) % 4
    n = m + 1 + (-shift - q) // 4
    if 0 <= n <= 4:
        return chunks[index, :, 640 * q + 128 * n : 640 * q + 128 * n + 128]
    return jnp.zeros((16, 128), BF)


def weights(chunks, indices, shifts, lanes):
    return jnp.concatenate(
        [
            jnp.concatenate(
                [place(chunks, i, shift, m) for i in indices for m in range(lanes // 128)],
                axis=1,
            )
            for shift in shifts
        ],
        axis=0,
    )


def moves(c, size):
    r, l = iota((128, 128), 0), iota((128, 128), 1)
    at = l % size
    ahead = (r == l + c) & (at + c < size)
    behind = ((r == l + c) & (at < size - 4)) | ((r == l + c - size) & (at + c >= size))
    return jnp.concatenate(
        [jnp.where(behind, 1.0, 0.0), jnp.where(ahead, 1.0, 0.0)], axis=1
    ).astype(BF)


def gather(parts, size):
    at = iota(parts[0].shape, 1) % size
    value = parts[2] + jnp.where(at < size - 4, roll(parts[3], -4), 0.0)
    value += jnp.where(at >= 4, roll(parts[1], 4), roll(parts[1], 4 - size))
    back = jnp.where(at >= 4, roll(parts[0], 8 - size), 0.0)
    return value + jnp.where(at >= 8, roll(parts[0], 8), back)


def kernel(
    count_x, count_y,
    charges_in, k_fine, k_mid, k_top, out,
    charges, own, edge, xl, xr, yl, yr, corner,
    mid_pack, mid_edge, mxl, mxr, myl, myr, mid_corner,
    top_pack, top_in,
    taps_in, taps, chunks, inner, outer, acc, mid_acc, top_acc, mid_right, top_right,
    rows_mid, rows_top, zx, pxy, pz,
    load_sem, send_sem, recv_sem,
):
    gx, gy = lax.axis_index("gx"), lax.axis_index("gy")

    def valid(dx, dy):
        ok = jnp.bool_(True)
        if dx:
            ok = (gx + dx >= 0) & (gx + dx < count_x)
        if dy:
            ok = ok & (gy + dy >= 0) & (gy + dy < count_y)
        return ok

    load = pltpu.make_async_copy(charges_in, charges, load_sem)
    load.start()

    @pl.when((gx < 2) | (gx >= count_x - 2) | (gy == 0) | (gy == count_y - 1))
    def _():
        for ref in (yl, yr, corner, mxl, mxr, myl, myr, mid_corner, top_in):
            ref[...] = jnp.zeros_like(ref)

    for ref, dx in ((xl, -1), (xr, 1)):

        @pl.when(~valid(dx, 0))
        def _(ref=ref):
            ref[...] = jnp.zeros_like(ref)

    for ref in (xl.at[0], xr.at[7], mxl.at[0]):
        ref[...] = jnp.zeros(ref.shape, BF)
    barrier = pltpu.get_barrier_semaphore()
    for dx, dy in TOPS:

        @pl.when(valid(dx, dy))
        def _(dx=dx, dy=dy):
            pl.semaphore_signal(
                barrier, inc=1, device_id=(gx + dx, gy + dy), device_id_type=MESH
            )

    taps_in[...] = jnp.zeros_like(taps_in)
    for level, ref in enumerate((k_fine, k_mid, k_top)):
        taps_in[level, :, 0:15, 0:15] = ref[...].astype(F32)
    flat = sum(roll(taps_in[level], 16 * level + 1) for level in range(3))
    flat = flat.reshape(240, 128).astype(BF)
    lane_of = iota((240, 512), 0)
    lane_of = (lane_of // 16) * 32 + lane_of % 16
    spread = jnp.where(lane_of == iota((240, 512), 1), 1.0, 0.0).astype(BF)
    taps[...] = lax.dot_general(
        flat, spread, (((0,), (0,)), ((), ())), preferred_element_type=F32
    )[0:48]

    load.wait()
    own[...] = charges[...].astype(BF)
    edge[0] = charges[:, 0:8, :].reshape(12, 16, 128).astype(BF)
    edge[1] = charges[:, 56:64, :].reshape(12, 16, 128).astype(BF)

    def build(row):
        chunks[row] = toeplitz_chunks(taps[pl.ds(row, 1), :])

    messages = {
        "x_near": (own.at[20:24], xl.at[4:8]),
        "x_far": (own.at[17:20], xl.at[1:4]),
        "x_lo": (own.at[0:7], xr.at[0:7]),
        "y_hi": (edge.at[1], yl),
        "y_lo": (edge.at[0], yr),
        "c_hh": (edge.at[1, 8:12], corner.at[0]),
        "c_hl": (edge.at[0, 8:12], corner.at[1]),
        "c_lh": (edge.at[1, 0:4], corner.at[2]),
        "c_ll": (edge.at[0, 0:4], corner.at[3]),
    }
    copies = {}

    def describe(key, source, target, direction):
        dx, dy = direction
        n = len(copies)
        copies[key] = (
            pltpu.make_async_remote_copy(
                src_ref=source,
                dst_ref=target,
                send_sem=send_sem.at[n],
                recv_sem=recv_sem.at[n],
                device_id=(gx + dx, gy + dy),
                device_id_type=MESH,
            ),
            direction,
        )

    def start(key):
        copy, (dx, dy) = copies[key]

        @pl.when(valid(dx, dy))
        def _():
            copy.start()

    def arrived(key):
        copy, (dx, dy) = copies[key]

        @pl.when(valid(-dx, -dy))
        def _():
            copy.wait_recv()

    def sent(key):
        copy, (dx, dy) = copies[key]

        @pl.when(valid(dx, dy))
        def _():
            copy.wait_send()

    for key, direction in ROUND1:
        describe(key, *messages[key], direction)

    def shift_rows(value, x, target):
        rows = value.shape[0]
        lane = iota((rows, 128), 1)
        for c in range(4):
            turned = roll(value, -c)
            ahead = jnp.where(lane + c < 128, turned, 0.0) if c else turned
            behind = jnp.where((lane < 124) | (lane + c >= 128), turned, 0.0)
            target[1, c, x] = ahead.astype(BF)
            target[0, c, x] = behind.astype(BF)

    def window(side, c, k, t):
        group = pl.ds(8 * k, 8)
        if t == 0:
            parts = [outer[0, side, c, group], inner[side, c, group, 0:16, :]]
        elif t == 3:
            parts = [inner[side, c, group, 32:48, :], outer[1, side, c, group]]
        else:
            parts = [inner[side, c, group, 16 * t - 16 : 16 * t + 16, :]]
        return jnp.concatenate(parts, axis=1).reshape(256, 128)

    def fine_product(s, p, k):
        lo, hi, first = BANDS[k]
        left = weights(
            chunks, [4 * s + c for c in range(4)], range(first - 14, first - 14 + hi - lo), 256
        )
        right = jnp.concatenate(
            [
                jnp.concatenate([window(s // 2, c, k, t) for t in PAIRS[p]], axis=1)
                for c in range(4)
            ],
            axis=0,
        )
        return dot(left, right)

    def fine_centre(s, p):
        one, two, three = (fine_product(s, p, k) for k in (1, 2, 3))
        acc[s, p, 0:16] = one[0:16]
        acc[s, p, 16:144] = one[16:144] + two[0:128]
        acc[s, p, 144:240] = one[144:240] + two[128:224] + three[0:96]
        acc[s, p, 240:368] = two[224:352] + three[96:224]
        acc[s, p, 368:384] = three[224:240]

    def first_steps(n, _):
        for h in range(2):
            build(2 * n + h)
        for h in range(3):
            x = 3 * n + h
            shift_rows(charges[x, 8:56, :], x + 8, inner)
        return 0

    in_x = 1 + jnp.minimum(gx, 2) + jnp.minimum(count_x - 1 - gx, 2)
    in_y = 1 + jnp.minimum(gy, 1) + jnp.minimum(count_y - 1 - gy, 1)
    pl.semaphore_wait(barrier, in_x * in_y - 1)
    for key in EARLY:
        start(key)
    lax.fori_loop(0, 8, first_steps, 0)
    for key in LATE:
        start(key)

    def second_steps(s, _):
        fine_centre(s, 0)
        for h in range(8):
            build(16 + 8 * s + h)
        return 0

    lax.fori_loop(0, 4, second_steps, 0)

    r, c = iota((384, 256), 0), iota((384, 256), 1)
    pxy[...] = (near(r // 16, c // 16) * near(r % 16, c % 16)).astype(BF)
    for p in range(2):
        r, c = iota((256, 256), 0), iota((256, 256), 1)
        block = r // 64
        block = jnp.where(block == 1, 2, jnp.where(block == 2, 1, block))
        column_of = jnp.where(c < 128, PAIRS[p][0], PAIRS[p][1])
        pz[p] = jnp.where(block == column_of, near(c % 128, r % 64), 0.0).astype(BF)

    for key in ("x_near", "y_hi", "c_hh"):
        arrived(key)
    r, c = iota((128, 128), 0), iota((128, 128), 1)
    halve = near(r, c % 64).astype(BF)
    quarter = jnp.where(r < 64, near(r, c % 32), 0.0).astype(BF)
    side_rows = yl[...].astype(F32).reshape(24, 8, 128)
    body = jnp.concatenate([side_rows, charges[...]], axis=1).reshape(24 * 72, 128)
    zx[4:28] = dot(body.astype(BF), halve).reshape(24, 72, 128)
    side_rows = corner[0].astype(F32).reshape(8, 8, 128)[4:8]
    body = jnp.concatenate([side_rows, xl[4:8].astype(F32)], axis=1).reshape(4 * 72, 128)
    zx[0:4] = dot(body.astype(BF), halve).reshape(4, 72, 128)
    rows_mid[:, 0:16, :] = jnp.zeros((13, 16, 128), F32)
    for i in range(13):
        rows_mid[i, 16:88, :] = (
            0.5 * zx[2 * i + 1] + zx[2 * i + 2] + 0.5 * zx[2 * i + 3]
        )
    mid = (
        0.5 * rows_mid[:, pl.ds(7, 40, 2), :]
        + rows_mid[:, pl.ds(8, 40, 2), :]
        + 0.5 * rows_mid[:, pl.ds(9, 40, 2), :]
    ).astype(BF)
    mid_rows = mid.astype(F32)
    lane = iota((12, 16, 128), 2)
    packed = jnp.where(lane < 64, mid_rows[1:13, 8:24], mid_rows[1:13, 24:40])
    mid_pack[...] = packed.astype(BF)
    mid_edge[0] = packed[:, 0:8].reshape(6, 16, 128).astype(BF)
    mid_edge[1] = packed[:, 8:16].reshape(6, 16, 128).astype(BF)

    mid_messages = {
        (1, 0): (mid_pack.at[5:12], mxl.at[1:8]),
        (-1, 0): (mid_pack.at[0:8], mxr),
        (0, 1): (mid_edge.at[1], myl),
        (0, -1): (mid_edge.at[0], myr),
        (1, 1): (mid_edge.at[1, 2:6], mid_corner.at[0]),
        (1, -1): (mid_edge.at[0, 2:6], mid_corner.at[1]),
        (-1, 1): (mid_edge.at[1, 0:4], mid_corner.at[2]),
        (-1, -1): (mid_edge.at[0, 0:4], mid_corner.at[3]),
    }
    for direction in MIDS:
        describe(("mid", direction), *mid_messages[direction], direction)
        start(("mid", direction))

    zt = dot(mid_rows.reshape(520, 128).astype(BF), quarter).reshape(13, 40, 128)
    for i in range(6):
        rows_top[i] = 0.5 * zt[2 * i] + zt[2 * i + 1] + 0.5 * zt[2 * i + 2]
    top = (
        0.5 * rows_top[:, pl.ds(7, 16, 2), :]
        + rows_top[:, pl.ds(8, 16, 2), :]
        + 0.5 * rows_top[:, pl.ds(9, 16, 2), :]
    )
    lane = iota((6, 8, 128), 2)
    packed = jnp.where(lane % 64 < 32, top[:, 0:8], top[:, 8:16])
    top_pack[...] = packed.reshape(3, 16, 128).astype(BF)
    for direction in TOPS:
        dx, dy = direction
        part = {2: slice(2, 3), -2: slice(0, 1)}.get(dx, slice(0, 3))
        target = top_in.at[2 - dx, 1 - dy, part]
        describe(("top", direction), top_pack.at[part], target, direction)
        start(("top", direction))

    arrived("y_lo")

    def outer_columns(n, _):
        low, high = yl[n].astype(F32), yr[n].astype(F32)
        for h in range(2):
            x = 2 * n + h
            shift_rows(
                jnp.concatenate([low[8 * h : 8 * h + 8], charges[x, 0:8, :]], axis=0),
                x + 8,
                outer.at[0],
            )
            shift_rows(
                jnp.concatenate([charges[x, 56:64, :], high[8 * h : 8 * h + 8]], axis=0),
                x + 8,
                outer.at[1],
            )
        return 0

    lax.fori_loop(0, 12, outer_columns, 0, unroll=2)

    def third_steps(s, _):
        fine_centre(s, 1)
        return 0

    lax.fori_loop(0, 4, third_steps, 0)

    for key in ("x_far", "x_lo", "c_hl", "c_lh", "c_ll"):
        arrived(key)

    def outer_rows(n, _):
        for side, rows in ((0, xl), (1, xr)):
            low = corner[2 * side, n].astype(F32)
            high = corner[2 * side + 1, n].astype(F32)
            for h in range(2):
                x = 2 * n + h
                target = x + 32 * side
                row = rows[x].astype(F32)
                part = slice(8 * h, 8 * h + 8)
                shift_rows(row[8:56], target, inner)
                shift_rows(jnp.concatenate([low[part], row[0:8]], axis=0), target, outer.at[0])
                shift_rows(jnp.concatenate([row[56:64], high[part]], axis=0), target, outer.at[1])
        return 0

    lax.fori_loop(0, 4, outer_rows, 0)

    def fourth_steps(s, _):
        for p in range(2):
            for k in (0, 4):
                lo, hi, _ = BANDS[k]
                acc[s, p, 16 * lo : 16 * hi, :] += fine_product(s, p, k)
        return 0

    lax.fori_loop(0, 4, fourth_steps, 0)

    def mid_field(centre, low, high):
        lane = iota(low.shape, 2)
        first = roll(jnp.where(lane < 64, centre[:, 8:16], low), 64)
        last = roll(jnp.where(lane < 64, high, centre[:, 0:8]), 64)
        field = jnp.concatenate([first, centre, last], axis=1)
        return field.reshape(32 * field.shape[0], 128).astype(BF)

    def mid_shift(field, start):
        rows = field.shape[0]
        for c in range(4):
            moved = dot(field, moves(c, 64)).reshape(rows // 32, 32, 256)
            turned = jnp.concatenate([moved[:, 8:32], moved[:, 0:8]], axis=1)
            for side in range(2):
                lanes = slice(128 * side, 128 * side + 128)
                both = jnp.concatenate([moved[:, :, lanes], turned[:, :, lanes]], axis=2)
                mid_right[side, c, start : start + rows, :] = both.reshape(rows, 256).astype(BF)

    def mid_product(s, blocks, start, rows):
        left = weights(
            chunks,
            [16 + 4 * s + c for c in range(4)],
            [i + 1 - start // 32 for i in blocks],
            rows,
        )
        right = jnp.concatenate(
            [mid_right[s // 2, c, start : start + rows, :] for c in range(4)], axis=0
        )
        return dot(left, right)

    def pairs(ref):
        value = ref[...].astype(F32)
        return value.reshape(2 * value.shape[0], 8, 128)

    for direction in ((0, 1), (0, -1)):
        arrived(("mid", direction))
    mid_shift(mid_field(mid_pack[...].astype(F32), pairs(myl), pairs(myr)), 256)

    def fifth_steps(s, _):
        mid_acc[s] = mid_product(s, range(13), 256, 384)
        return 0

    lax.fori_loop(0, 4, fifth_steps, 0)

    for direction in MIDS:
        if direction[0]:
            arrived(("mid", direction))
    for side, rows in ((0, mxl), (1, mxr)):
        low, high = pairs(mid_corner.at[2 * side]), pairs(mid_corner.at[2 * side + 1])
        mid_shift(mid_field(rows[...].astype(F32), low, high), 640 * side)

    for direction in TOPS:
        arrived(("top", direction))

    def strip(dy):
        parts = []
        for dx in (-2, -1, 0, 1, 2):
            if dx == 0 and dy == 0:
                ref = top_pack
            elif dx == -2:
                ref = top_in.at[0, 1 + dy, 2:3]
            elif dx == 2:
                ref = top_in.at[4, 1 + dy, 0:1]
            else:
                ref = top_in.at[2 + dx, 1 + dy]
            parts.append(pairs(ref))
        return jnp.concatenate(parts, axis=0)

    centre, low, high = strip(0), strip(-1), strip(1)
    lane = iota((22, 8, 128), 2) % 64
    low = roll(jnp.where(lane < 32, centre, low), 32)
    high = roll(jnp.where(lane < 32, high, centre), 32)
    field = jnp.concatenate([low, centre, high], axis=1).reshape(528, 128).astype(BF)
    lane = iota((20, 24, 128), 2)
    for c in range(4):
        moved = dot(field, moves(c, 32)).reshape(22, 24, 256)
        moved = jnp.concatenate([moved, jnp.zeros((2, 24, 256), F32)], axis=0)
        for side in range(2):
            part = moved[:, :, 128 * side : 128 * side + 128]
            both = jnp.where(lane < 64, part[0:20], part[4:24])
            both = jnp.concatenate([both, jnp.zeros((20, 8, 128), F32)], axis=1)
            top_right[side, c] = both.reshape(640, 128).astype(BF)

    def sixth_steps(s, _):
        mid_acc[s, 0:112, :] += mid_product(s, range(7), 0, 256)
        mid_acc[s, 80:208, :] += mid_product(s, range(5, 13), 640, 256)
        left = weights(chunks, [32 + 4 * s + c for c in range(4)], range(1, 5), 640)
        right = jnp.concatenate([top_right[s // 2, c] for c in range(4)], axis=0)
        top_acc[s] = dot(left, right)
        return 0

    lax.fori_loop(0, 4, sixth_steps, 0)

    last_x, last_y = gx == count_x - 1, gy == count_y - 1
    r, c = iota((128, 128), 0), iota((128, 128), 1)
    beyond = (last_x & (r // 16 == 6)) | (last_y & (r % 16 == 8) & (c % 64 >= 32))
    top_e = gather([top_acc[s] for s in range(4)], 32)
    top_e = jnp.concatenate([top_e, roll(top_e, 64)], axis=0)
    high, low = split(jnp.where(beyond, 0.0, top_e))
    stretch = jnp.where(
        (r < 64) & (r // 32 == c // 64), near(c % 64, r % 32), 0.0
    ).astype(BF)
    wide = dot(
        jnp.concatenate([high, low], axis=1), jnp.concatenate([stretch, stretch], axis=0)
    )
    wide = jnp.concatenate(split(wide), axis=0)
    r, c = iota((208, 128), 0), iota((208, 128), 1)
    along_x = near(r // 16, c // 16)
    parts = []
    for parity in range(2):
        spread = (along_x * near(8 * parity + r % 16, c % 16)).astype(BF)
        parts.append(dot(jnp.concatenate([spread, spread], axis=1), wide))
    mid_u = gather([mid_acc[s] for s in range(4)], 64) + jnp.concatenate(parts, axis=1)

    r, c = iota((208, 256), 0), iota((208, 256), 1)
    beyond = (last_x & (r // 16 == 12)) | (last_y & (r % 16 == 8) & (c >= 192))
    mid_u = jnp.concatenate(split(jnp.where(beyond, 0.0, mid_u)), axis=1)
    spread = jnp.concatenate([pxy[...], pxy[...]], axis=1)
    lane = iota((384, 128), 1)
    for p in range(2):
        wide = dot(mid_u, jnp.concatenate([pz[p], pz[p]], axis=0))
        high, low = split(jnp.concatenate([wide, jnp.zeros((48, 256), F32)], axis=0))
        total = dot(spread, jnp.concatenate([high, low], axis=0))
        for h in range(2):
            lanes = slice(128 * h, 128 * h + 128)
            value = total[:, lanes] + acc[2, p, :, lanes]
            value += jnp.where(lane < 124, roll(acc[3, p, :, lanes], -4), 0.0)
            value += roll(acc[1, p, :, lanes], 4)
            value += jnp.where(lane >= 4, roll(acc[0, p, :, lanes], 8), 0.0)
            t = PAIRS[p][h]
            out[:, 16 * t : 16 * t + 16, :] = value.reshape(24, 16, 128)

    for key in copies:
        sent(key)


def solution(mesh):
    count_x, count_y = mesh.shape["gx"], mesh.shape["gy"]
    vmem = pl.BlockSpec(memory_space=pltpu.VMEM)
    messages = len(ROUND1) + len(MIDS) + len(TOPS)

    def shards(charges, kernel_fine, kernel_mid, kernel_top):
        return pl.pallas_call(
            functools.partial(kernel, count_x, count_y),
            out_shape=pltpu.VMEM(charges.shape, F32),
            in_specs=[pl.BlockSpec(memory_space=pl.ANY)] + [vmem] * 3,
            out_specs=vmem,
            scratch_shapes=[
                pltpu.VMEM((24, 64, 128), F32),
                pltpu.VMEM((24, 64, 128), BF),
                pltpu.VMEM((2, 12, 16, 128), BF),
                pltpu.VMEM((8, 64, 128), BF),
                pltpu.VMEM((8, 64, 128), BF),
                pltpu.VMEM((12, 16, 128), BF),
                pltpu.VMEM((12, 16, 128), BF),
                pltpu.VMEM((4, 4, 16, 128), BF),
                pltpu.VMEM((12, 16, 128), BF),
                pltpu.VMEM((2, 6, 16, 128), BF),
                pltpu.VMEM((8, 16, 128), BF),
                pltpu.VMEM((8, 16, 128), BF),
                pltpu.VMEM((6, 16, 128), BF),
                pltpu.VMEM((6, 16, 128), BF),
                pltpu.VMEM((4, 4, 16, 128), BF),
                pltpu.VMEM((3, 16, 128), BF),
                pltpu.VMEM((5, 3, 3, 16, 128), BF),
                pltpu.VMEM((3, 15, 16, 128), F32),
                pltpu.VMEM((48, 512), F32),
                pltpu.VMEM((48, 16, 2560), BF),
                pltpu.VMEM((2, 4, 40, 48, 128), BF),
                pltpu.VMEM((2, 2, 4, 40, 16, 128), BF),
                pltpu.VMEM((4, 2, 384, 256), F32),
                pltpu.VMEM((4, 208, 256), F32),
                pltpu.VMEM((4, 64, 128), F32),
                pltpu.VMEM((2, 4, 896, 256), BF),
                pltpu.VMEM((2, 4, 640, 128), BF),
                pltpu.VMEM((13, 88, 128), F32),
                pltpu.VMEM((6, 40, 128), F32),
                pltpu.VMEM((28, 72, 128), F32),
                pltpu.VMEM((384, 256), BF),
                pltpu.VMEM((2, 256, 256), BF),
                pltpu.SemaphoreType.DMA,
                pltpu.SemaphoreType.DMA((messages,)),
                pltpu.SemaphoreType.DMA((messages,)),
            ],
            compiler_params=pltpu.CompilerParams(
                collective_id=0, has_side_effects=True, vmem_limit_bytes=56 * 2**20
            ),
        )(charges, kernel_fine, kernel_mid, kernel_top)

    placed = (P("gx", "gy", None), P(), P(), P())
    return jax.shard_map(
        shards, mesh=mesh, in_specs=placed, out_specs=P("gx", "gy", None), check_vma=False
    )
```

```python
import functools

import jax
import jax.numpy as jnp
from jax import lax
from jax.experimental import pallas as pl
from jax.experimental.pallas import tpu as pltpu
from jax.sharding import PartitionSpec as P

MESH = pl.DeviceIdType.MESH
BF, F32 = jnp.bfloat16, jnp.float32

BANDS = ((0, 7, 15), (0, 15, 7), (1, 23, 0), (9, 24, 0), (17, 24, 0))
PAIRS = ((1, 2), (0, 3))
MID_WINDOWS = (0, 2, 1, 3)

ROUND1 = (
    ("x_near", (1, 0)),
    ("y_hi", (0, 1)),
    ("c_hh", (1, 1)),
    ("y_lo", (0, -1)),
    ("x_far", (1, 0)),
    ("x_lo", (-1, 0)),
    ("c_hl", (1, -1)),
    ("c_lh", (-1, 1)),
    ("c_ll", (-1, -1)),
)
EARLY = ("x_near", "y_hi", "c_hh", "y_lo", "x_far", "x_lo", "c_hl", "c_lh", "c_ll")
LATE = ()
MIDS = tuple((dx, dy) for dx in (-1, 0, 1) for dy in (-1, 0, 1) if (dx, dy) != (0, 0))
TOPS = tuple(
    (dx, dy) for dx in (-1, 1, -2, 2, 0) for dy in (0, -1, 1) if (dx, dy) != (0, 0)
)


def iota(shape, dim):
    return lax.broadcasted_iota(jnp.int32, shape, dim)


def dot(a, b):
    return jnp.dot(a, b, preferred_element_type=F32)


def near(twice, other):
    gap = jnp.abs(twice - 2 * other)
    return jnp.where(gap == 0, 1.0, jnp.where(gap == 1, 0.5, 0.0)).astype(F32)


def split(value):
    high = value.astype(BF)
    return high, (value - high.astype(F32)).astype(BF)


def roll(value, shift):
    size = value.shape[-1]
    return value if shift % size == 0 else pltpu.roll(value, shift % size, axis=value.ndim - 1)


def toeplitz_chunks(row):
    block = pltpu.roll(
        jnp.broadcast_to(row, (16, 512)), 1, axis=1, stride=1, stride_axis=0
    )
    block = jnp.concatenate([jnp.zeros((16, 128), F32), block], axis=1)
    return jnp.concatenate([roll(block, -32 * q).astype(BF) for q in range(4)], axis=1)


def place(chunks, index, shift, m):
    q = (-shift) % 4
    n = m + 1 + (-shift - q) // 4
    if 0 <= n <= 4:
        return chunks[index, :, 640 * q + 128 * n : 640 * q + 128 * n + 128]
    return jnp.zeros((16, 128), BF)


def weights(chunks, indices, shifts, lanes):
    return jnp.concatenate(
        [
            jnp.concatenate(
                [place(chunks, i, shift, m) for i in indices for m in range(lanes // 128)],
                axis=1,
            )
            for shift in shifts
        ],
        axis=0,
    )


def terms(s):
    return (1, 2, 3) if isinstance(s, int) and s == 0 else (0, 1, 2, 3)


def each_sum(body):
    body(0)

    def step(s, _):
        body(s)
        return 0

    lax.fori_loop(1, 4, step, 0)


def moves(c, size):
    r, l = iota((128, 128), 0), iota((128, 128), 1)
    at = l % size
    ahead = (r == l + c) & (at + c < size)
    behind = ((r == l + c) & (at < size - 4)) | ((r == l + c - size) & (at + c >= size))
    return jnp.concatenate(
        [jnp.where(behind, 1.0, 0.0), jnp.where(ahead, 1.0, 0.0)], axis=1
    ).astype(BF)


def gather(parts, size):
    at = iota(parts[0].shape, 1) % size
    value = parts[2] + jnp.where(at < size - 4, roll(parts[3], -4), 0.0)
    value += jnp.where(at >= 4, roll(parts[1], 4), roll(parts[1], 4 - size))
    back = jnp.where(at >= 4, roll(parts[0], 8 - size), 0.0)
    return value + jnp.where(at >= 8, roll(parts[0], 8), back)


def kernel(
    count_x, count_y,
    charges_in, k_fine, k_mid, k_top, out,
    charges, own, edge, xl, xr, yl, yr, corner,
    mid_pack, mid_edge, mxl, mxr, myl, myr, mid_corner,
    top_pack, top_in,
    taps_in, taps, chunks, inner, outer, acc, mid_acc, top_acc, mid_right, top_right,
    rows_mid, rows_top, zx, pxy, pz,
    load_sem, send_sem, recv_sem,
):
    gx, gy = lax.axis_index("gx"), lax.axis_index("gy")

    def valid(dx, dy):
        ok = jnp.bool_(True)
        if dx:
            ok = (gx + dx >= 0) & (gx + dx < count_x)
        if dy:
            ok = ok & (gy + dy >= 0) & (gy + dy < count_y)
        return ok

    load = pltpu.make_async_copy(charges_in, charges, load_sem)
    load.start()

    @pl.when((gx < 2) | (gx >= count_x - 2) | (gy == 0) | (gy == count_y - 1))
    def _():
        for ref in (yl, yr, corner, mxl, mxr, myl, myr, mid_corner, top_in):
            ref[...] = jnp.zeros_like(ref)

    for ref, dx in ((xl, -1), (xr, 1)):

        @pl.when(~valid(dx, 0))
        def _(ref=ref):
            ref[...] = jnp.zeros_like(ref)

    for ref in (xl.at[0], xr.at[7], mxl.at[0]):
        ref[...] = jnp.zeros(ref.shape, BF)
    barrier = pltpu.get_barrier_semaphore()
    for dx, dy in TOPS:

        @pl.when(valid(dx, dy))
        def _(dx=dx, dy=dy):
            pl.semaphore_signal(
                barrier, inc=1, device_id=(gx + dx, gy + dy), device_id_type=MESH
            )

    taps_in[...] = jnp.zeros_like(taps_in)
    for level, ref in enumerate((k_fine, k_mid, k_top)):
        taps_in[level, :, 0:15, 0:15] = ref[...].astype(F32)
    flat = sum(roll(taps_in[level], 16 * level + 1) for level in range(3))
    flat = flat.reshape(240, 128).astype(BF)
    lane_of = iota((240, 512), 0)
    lane_of = (lane_of // 16) * 32 + lane_of % 16
    spread = jnp.where(lane_of == iota((240, 512), 1), 1.0, 0.0).astype(BF)
    taps[...] = lax.dot_general(
        flat, spread, (((0,), (0,)), ((), ())), preferred_element_type=F32
    )[0:48]

    load.wait()
    own[...] = charges[...].astype(BF)
    edge[0] = charges[:, 0:8, :].reshape(12, 16, 128).astype(BF)
    edge[1] = charges[:, 56:64, :].reshape(12, 16, 128).astype(BF)

    def build(row):
        chunks[row] = toeplitz_chunks(taps[pl.ds(row, 1), :])

    messages = {
        "x_near": (own.at[20:24], xl.at[4:8]),
        "x_far": (own.at[17:20], xl.at[1:4]),
        "x_lo": (own.at[0:7], xr.at[0:7]),
        "y_hi": (edge.at[1], yl),
        "y_lo": (edge.at[0], yr),
        "c_hh": (edge.at[1, 8:12], corner.at[0]),
        "c_hl": (edge.at[0, 8:12], corner.at[1]),
        "c_lh": (edge.at[1, 0:4], corner.at[2]),
        "c_ll": (edge.at[0, 0:4], corner.at[3]),
    }
    copies = {}

    def describe(key, source, target, direction):
        dx, dy = direction
        n = len(copies)
        copies[key] = (
            pltpu.make_async_remote_copy(
                src_ref=source,
                dst_ref=target,
                send_sem=send_sem.at[n],
                recv_sem=recv_sem.at[n],
                device_id=(gx + dx, gy + dy),
                device_id_type=MESH,
            ),
            direction,
        )

    def start(key):
        copy, (dx, dy) = copies[key]

        @pl.when(valid(dx, dy))
        def _():
            copy.start()

    def arrived(key):
        copy, (dx, dy) = copies[key]

        @pl.when(valid(-dx, -dy))
        def _():
            copy.wait_recv()

    def sent(key):
        copy, (dx, dy) = copies[key]

        @pl.when(valid(dx, dy))
        def _():
            copy.wait_send()

    for key, direction in ROUND1:
        describe(key, *messages[key], direction)

    def shift_rows(value, x, target):
        rows = value.shape[0]
        lane = iota((rows, 128), 1)
        for c in range(4):
            turned = roll(value, -c)
            ahead = jnp.where(lane + c < 128, turned, 0.0) if c else turned
            behind = jnp.where((lane < 124) | (lane + c >= 128), turned, 0.0)
            target[1, c, x] = ahead.astype(BF)
            target[0, c, x] = behind.astype(BF)

    def window(side, c, k, t):
        group = pl.ds(8 * k, 8)
        if t == 0:
            parts = [outer[0, side, c, group], inner[side, c, group, 0:16, :]]
        elif t == 3:
            parts = [inner[side, c, group, 32:48, :], outer[1, side, c, group]]
        else:
            parts = [inner[side, c, group, 16 * t - 16 : 16 * t + 16, :]]
        return jnp.concatenate(parts, axis=1).reshape(256, 128)

    def fine_product(s, p, k):
        lo, hi, first = BANDS[k]
        left = weights(
            chunks, [4 * s + c for c in terms(s)], range(first - 14, first - 14 + hi - lo), 256
        )
        right = jnp.concatenate(
            [
                jnp.concatenate([window(s // 2, c, k, t) for t in PAIRS[p]], axis=1)
                for c in terms(s)
            ],
            axis=0,
        )
        return dot(left, right)

    def fine_centre(s, p):
        one, two, three = (fine_product(s, p, k) for k in (1, 2, 3))
        acc[s, p, 0:16] = one[0:16]
        acc[s, p, 16:144] = one[16:144] + two[0:128]
        acc[s, p, 144:240] = one[144:240] + two[128:224] + three[0:96]
        acc[s, p, 240:368] = two[224:352] + three[96:224]
        acc[s, p, 368:384] = three[224:240]

    def first_steps(n, _):
        build(8 + n)
        for h in range(3):
            x = 3 * n + h
            shift_rows(charges[x, 8:56, :], x + 8, inner)
        return 0

    def fine_weights(n, _):
        for h in range(4):
            build(4 * n + h)
        return 0

    lax.fori_loop(0, 2, fine_weights, 0)

    in_x = 1 + jnp.minimum(gx, 2) + jnp.minimum(count_x - 1 - gx, 2)
    in_y = 1 + jnp.minimum(gy, 1) + jnp.minimum(count_y - 1 - gy, 1)
    pl.semaphore_wait(barrier, in_x * in_y - 1)
    for key in EARLY:
        start(key)
    lax.fori_loop(0, 8, first_steps, 0)
    for key in LATE:
        start(key)

    def second_steps(s):
        fine_centre(s, 0)
        for h in range(8):
            build(16 + 8 * s + h)

    each_sum(second_steps)

    r, c = iota((384, 256), 0), iota((384, 256), 1)
    pxy[...] = (near(r // 16, c // 16) * near(r % 16, c % 16)).astype(BF)
    for p in range(2):
        r, c = iota((256, 256), 0), iota((256, 256), 1)
        block = r // 64
        block = jnp.where(block == 1, 2, jnp.where(block == 2, 1, block))
        column_of = jnp.where(c < 128, PAIRS[p][0], PAIRS[p][1])
        pz[p] = jnp.where(block == column_of, near(c % 128, r % 64), 0.0).astype(BF)

    for key in ("x_near", "y_hi", "c_hh"):
        arrived(key)
    r, c = iota((128, 128), 0), iota((128, 128), 1)
    halve = near(r, c % 64).astype(BF)
    quarter = jnp.where(r < 64, near(r, c % 32), 0.0).astype(BF)
    side_rows = yl[...].astype(F32).reshape(24, 8, 128)
    body = jnp.concatenate([side_rows, charges[...]], axis=1).reshape(24 * 72, 128)
    zx[4:28] = dot(body.astype(BF), halve).reshape(24, 72, 128)
    side_rows = corner[0].astype(F32).reshape(8, 8, 128)[4:8]
    body = jnp.concatenate([side_rows, xl[4:8].astype(F32)], axis=1).reshape(4 * 72, 128)
    zx[0:4] = dot(body.astype(BF), halve).reshape(4, 72, 128)
    rows_mid[:, 0:16, :] = jnp.zeros((13, 16, 128), F32)
    for i in range(13):
        rows_mid[i, 16:88, :] = (
            0.5 * zx[2 * i + 1] + zx[2 * i + 2] + 0.5 * zx[2 * i + 3]
        )
    mid = (
        0.5 * rows_mid[:, pl.ds(7, 40, 2), :]
        + rows_mid[:, pl.ds(8, 40, 2), :]
        + 0.5 * rows_mid[:, pl.ds(9, 40, 2), :]
    ).astype(BF)
    mid_rows = mid.astype(F32)
    lane = iota((12, 16, 128), 2)
    packed = jnp.where(lane < 64, mid_rows[1:13, 8:24], mid_rows[1:13, 24:40])
    mid_pack[...] = packed.astype(BF)
    mid_edge[0] = packed[:, 0:8].reshape(6, 16, 128).astype(BF)
    mid_edge[1] = packed[:, 8:16].reshape(6, 16, 128).astype(BF)

    mid_messages = {
        (1, 0): (mid_pack.at[5:12], mxl.at[1:8]),
        (-1, 0): (mid_pack.at[0:8], mxr),
        (0, 1): (mid_edge.at[1], myl),
        (0, -1): (mid_edge.at[0], myr),
        (1, 1): (mid_edge.at[1, 2:6], mid_corner.at[0]),
        (1, -1): (mid_edge.at[0, 2:6], mid_corner.at[1]),
        (-1, 1): (mid_edge.at[1, 0:4], mid_corner.at[2]),
        (-1, -1): (mid_edge.at[0, 0:4], mid_corner.at[3]),
    }
    for direction in MIDS:
        describe(("mid", direction), *mid_messages[direction], direction)
        start(("mid", direction))

    zt = dot(mid_rows.reshape(520, 128).astype(BF), quarter).reshape(13, 40, 128)
    for i in range(6):
        rows_top[i] = 0.5 * zt[2 * i] + zt[2 * i + 1] + 0.5 * zt[2 * i + 2]
    top = (
        0.5 * rows_top[:, pl.ds(7, 16, 2), :]
        + rows_top[:, pl.ds(8, 16, 2), :]
        + 0.5 * rows_top[:, pl.ds(9, 16, 2), :]
    )
    lane = iota((6, 8, 128), 2)
    packed = jnp.where(lane % 64 < 32, top[:, 0:8], top[:, 8:16])
    top_pack[...] = packed.reshape(3, 16, 128).astype(BF)
    for direction in TOPS:
        dx, dy = direction
        part = {2: slice(2, 3), -2: slice(0, 1)}.get(dx, slice(0, 3))
        target = top_in.at[2 - dx, 1 - dy, part]
        describe(("top", direction), top_pack.at[part], target, direction)
        start(("top", direction))

    arrived("y_lo")

    def outer_columns(n, _):
        low, high = yl[n].astype(F32), yr[n].astype(F32)
        for h in range(2):
            x = 2 * n + h
            shift_rows(
                jnp.concatenate([low[8 * h : 8 * h + 8], charges[x, 0:8, :]], axis=0),
                x + 8,
                outer.at[0],
            )
            shift_rows(
                jnp.concatenate([charges[x, 56:64, :], high[8 * h : 8 * h + 8]], axis=0),
                x + 8,
                outer.at[1],
            )
        return 0

    lax.fori_loop(0, 12, outer_columns, 0, unroll=2)

    def third_steps(s):
        fine_centre(s, 1)

    each_sum(third_steps)

    for key in ("x_far", "x_lo", "c_hl", "c_lh", "c_ll"):
        arrived(key)

    def outer_rows(n, _):
        for side, rows in ((0, xl), (1, xr)):
            low = corner[2 * side, n].astype(F32)
            high = corner[2 * side + 1, n].astype(F32)
            for h in range(2):
                x = 2 * n + h
                target = x + 32 * side
                row = rows[x].astype(F32)
                part = slice(8 * h, 8 * h + 8)
                shift_rows(row[8:56], target, inner)
                shift_rows(jnp.concatenate([low[part], row[0:8]], axis=0), target, outer.at[0])
                shift_rows(jnp.concatenate([row[56:64], high[part]], axis=0), target, outer.at[1])
        return 0

    lax.fori_loop(0, 4, outer_rows, 0)

    def fourth_steps(s):
        for p in range(2):
            for k in (0, 4):
                lo, hi, _ = BANDS[k]
                acc[s, p, 16 * lo : 16 * hi, :] += fine_product(s, p, k)

    each_sum(fourth_steps)

    def mid_field(centre, low, high):
        lane = iota(low.shape, 2)
        first = roll(jnp.where(lane < 64, centre[:, 8:16], low), 64)
        last = roll(jnp.where(lane < 64, high, centre[:, 0:8]), 64)
        field = jnp.concatenate([first, centre, last], axis=1)
        return field.reshape(32 * field.shape[0], 128).astype(BF)

    def mid_shift(field, start):
        rows = field.shape[0]
        for c in range(4):
            moved = dot(field, moves(c, 64)).reshape(rows // 32, 32, 256)
            turned = jnp.concatenate([moved[:, 8:32], moved[:, 0:8]], axis=1)
            for side in range(2):
                lanes = slice(128 * side, 128 * side + 128)
                both = jnp.concatenate([moved[:, :, lanes], turned[:, :, lanes]], axis=2)
                mid_right[side, c, start : start + rows, :] = both.reshape(rows, 256).astype(BF)

    def mid_product(s, blocks, start, rows):
        left = weights(
            chunks,
            [16 + 4 * s + c for c in terms(s)],
            [i + 1 - start // 32 for i in blocks],
            rows,
        )
        right = jnp.concatenate(
            [mid_right[s // 2, c, start : start + rows, :] for c in terms(s)], axis=0
        )
        return dot(left, right)

    def pairs(ref):
        value = ref[...].astype(F32)
        return value.reshape(2 * value.shape[0], 8, 128)

    for direction in ((0, 1), (0, -1)):
        arrived(("mid", direction))
    mid_shift(mid_field(mid_pack[...].astype(F32), pairs(myl), pairs(myr)), 256)

    def fifth_steps(s):
        mid_acc[s] = mid_product(s, range(13), 256, 384)

    each_sum(fifth_steps)

    for direction in MIDS:
        if direction[0]:
            arrived(("mid", direction))
    for side, rows in ((0, mxl), (1, mxr)):
        low, high = pairs(mid_corner.at[2 * side]), pairs(mid_corner.at[2 * side + 1])
        mid_shift(mid_field(rows[...].astype(F32), low, high), 640 * side)

    for direction in TOPS:
        arrived(("top", direction))

    def strip(dy):
        parts = []
        for dx in (-2, -1, 0, 1, 2):
            if dx == 0 and dy == 0:
                ref = top_pack
            elif dx == -2:
                ref = top_in.at[0, 1 + dy, 2:3]
            elif dx == 2:
                ref = top_in.at[4, 1 + dy, 0:1]
            else:
                ref = top_in.at[2 + dx, 1 + dy]
            parts.append(pairs(ref))
        return jnp.concatenate(parts, axis=0)

    centre, low, high = strip(0), strip(-1), strip(1)
    lane = iota((22, 8, 128), 2) % 64
    low = roll(jnp.where(lane < 32, centre, low), 32)
    high = roll(jnp.where(lane < 32, high, centre), 32)
    field = jnp.concatenate([low, centre, high], axis=1).reshape(528, 128).astype(BF)
    lane = iota((20, 24, 128), 2)
    for c in range(4):
        moved = dot(field, moves(c, 32)).reshape(22, 24, 256)
        moved = jnp.concatenate([moved, jnp.zeros((2, 24, 256), F32)], axis=0)
        for side in range(2):
            part = moved[:, :, 128 * side : 128 * side + 128]
            both = jnp.where(lane < 64, part[0:20], part[4:24])
            both = jnp.concatenate([both, jnp.zeros((20, 8, 128), F32)], axis=1)
            top_right[side, c] = both.reshape(640, 128).astype(BF)

    def sixth_steps(s):
        mid_acc[s, 0:112, :] += mid_product(s, range(7), 0, 256)
        mid_acc[s, 80:208, :] += mid_product(s, range(5, 13), 640, 256)
        left = weights(chunks, [32 + 4 * s + c for c in terms(s)], range(1, 5), 640)
        right = jnp.concatenate([top_right[s // 2, c] for c in terms(s)], axis=0)
        top_acc[s] = dot(left, right)

    each_sum(sixth_steps)

    last_x, last_y = gx == count_x - 1, gy == count_y - 1
    r, c = iota((128, 128), 0), iota((128, 128), 1)
    beyond = (last_x & (r // 16 == 6)) | (last_y & (r % 16 == 8) & (c % 64 >= 32))
    top_e = gather([top_acc[s] for s in range(4)], 32)
    top_e = jnp.concatenate([top_e, roll(top_e, 64)], axis=0)
    high, low = split(jnp.where(beyond, 0.0, top_e))
    stretch = jnp.where(
        (r < 64) & (r // 32 == c // 64), near(c % 64, r % 32), 0.0
    ).astype(BF)
    wide = dot(
        jnp.concatenate([high, low], axis=1), jnp.concatenate([stretch, stretch], axis=0)
    )
    wide = jnp.concatenate(split(wide), axis=0)
    r, c = iota((208, 128), 0), iota((208, 128), 1)
    along_x = near(r // 16, c // 16)
    parts = []
    for parity in range(2):
        spread = (along_x * near(8 * parity + r % 16, c % 16)).astype(BF)
        parts.append(dot(jnp.concatenate([spread, spread], axis=1), wide))
    mid_u = gather([mid_acc[s] for s in range(4)], 64) + jnp.concatenate(parts, axis=1)

    r, c = iota((208, 256), 0), iota((208, 256), 1)
    beyond = (last_x & (r // 16 == 12)) | (last_y & (r % 16 == 8) & (c >= 192))
    mid_u = jnp.concatenate(split(jnp.where(beyond, 0.0, mid_u)), axis=1)
    spread = jnp.concatenate([pxy[...], pxy[...]], axis=1)
    lane = iota((384, 128), 1)
    for p in range(2):
        wide = dot(mid_u, jnp.concatenate([pz[p], pz[p]], axis=0))
        high, low = split(jnp.concatenate([wide, jnp.zeros((48, 256), F32)], axis=0))
        total = dot(spread, jnp.concatenate([high, low], axis=0))
        for h in range(2):
            lanes = slice(128 * h, 128 * h + 128)
            value = total[:, lanes] + acc[2, p, :, lanes]
            value += jnp.where(lane < 124, roll(acc[3, p, :, lanes], -4), 0.0)
            value += roll(acc[1, p, :, lanes], 4)
            value += jnp.where(lane >= 4, roll(acc[0, p, :, lanes], 8), 0.0)
            t = PAIRS[p][h]
            out[:, 16 * t : 16 * t + 16, :] = value.reshape(24, 16, 128)

    for key in copies:
        sent(key)


def solution(mesh):
    count_x, count_y = mesh.shape["gx"], mesh.shape["gy"]
    vmem = pl.BlockSpec(memory_space=pltpu.VMEM)
    messages = len(ROUND1) + len(MIDS) + len(TOPS)

    def shards(charges, kernel_fine, kernel_mid, kernel_top):
        return pl.pallas_call(
            functools.partial(kernel, count_x, count_y),
            out_shape=pltpu.VMEM(charges.shape, F32),
            in_specs=[pl.BlockSpec(memory_space=pl.ANY)] + [vmem] * 3,
            out_specs=vmem,
            scratch_shapes=[
                pltpu.VMEM((24, 64, 128), F32),
                pltpu.VMEM((24, 64, 128), BF),
                pltpu.VMEM((2, 12, 16, 128), BF),
                pltpu.VMEM((8, 64, 128), BF),
                pltpu.VMEM((8, 64, 128), BF),
                pltpu.VMEM((12, 16, 128), BF),
                pltpu.VMEM((12, 16, 128), BF),
                pltpu.VMEM((4, 4, 16, 128), BF),
                pltpu.VMEM((12, 16, 128), BF),
                pltpu.VMEM((2, 6, 16, 128), BF),
                pltpu.VMEM((8, 16, 128), BF),
                pltpu.VMEM((8, 16, 128), BF),
                pltpu.VMEM((6, 16, 128), BF),
                pltpu.VMEM((6, 16, 128), BF),
                pltpu.VMEM((4, 4, 16, 128), BF),
                pltpu.VMEM((3, 16, 128), BF),
                pltpu.VMEM((5, 3, 3, 16, 128), BF),
                pltpu.VMEM((3, 15, 16, 128), F32),
                pltpu.VMEM((48, 512), F32),
                pltpu.VMEM((48, 16, 2560), BF),
                pltpu.VMEM((2, 4, 40, 48, 128), BF),
                pltpu.VMEM((2, 2, 4, 40, 16, 128), BF),
                pltpu.VMEM((4, 2, 384, 256), F32),
                pltpu.VMEM((4, 208, 256), F32),
                pltpu.VMEM((4, 64, 128), F32),
                pltpu.VMEM((2, 4, 896, 256), BF),
                pltpu.VMEM((2, 4, 640, 128), BF),
                pltpu.VMEM((13, 88, 128), F32),
                pltpu.VMEM((6, 40, 128), F32),
                pltpu.VMEM((28, 72, 128), F32),
                pltpu.VMEM((384, 256), BF),
                pltpu.VMEM((2, 256, 256), BF),
                pltpu.SemaphoreType.DMA,
                pltpu.SemaphoreType.DMA((messages,)),
                pltpu.SemaphoreType.DMA((messages,)),
            ],
            compiler_params=pltpu.CompilerParams(
                collective_id=0, has_side_effects=True, vmem_limit_bytes=56 * 2**20
            ),
        )(charges, kernel_fine, kernel_mid, kernel_top)

    placed = (P("gx", "gy", None), P(), P(), P())
    return jax.shard_map(
        shards, mesh=mesh, in_specs=placed, out_specs=P("gx", "gy", None), check_vma=False
    )
```

```python
import functools

import jax
import jax.numpy as jnp
from jax import lax
from jax.experimental import pallas as pl
from jax.experimental.pallas import tpu as pltpu
from jax.sharding import PartitionSpec as P

MESH = pl.DeviceIdType.MESH
BF, F32 = jnp.bfloat16, jnp.float32

BANDS = ((0, 7, 15), (0, 15, 7), (1, 23, 0), (9, 24, 0), (17, 24, 0))
PAIRS = ((1, 2), (0, 3))
MID_WINDOWS = (0, 2, 1, 3)

ROUND1 = (
    ("x_near", (1, 0)),
    ("y_hi", (0, 1)),
    ("c_hh", (1, 1)),
    ("y_lo", (0, -1)),
    ("x_far", (1, 0)),
    ("x_lo", (-1, 0)),
    ("c_hl", (1, -1)),
    ("c_lh", (-1, 1)),
    ("c_ll", (-1, -1)),
)
EARLY = ("x_near", "y_hi", "c_hh", "y_lo", "x_far", "x_lo", "c_hl", "c_lh", "c_ll")
LATE = ()
MIDS = tuple((dx, dy) for dx in (-1, 0, 1) for dy in (-1, 0, 1) if (dx, dy) != (0, 0))
TOPS = tuple(
    (dx, dy) for dx in (-1, 1, -2, 2, 0) for dy in (0, -1, 1) if (dx, dy) != (0, 0)
)


def iota(shape, dim):
    return lax.broadcasted_iota(jnp.int32, shape, dim)


def dot(a, b):
    return jnp.dot(a, b, preferred_element_type=F32)


def near(twice, other):
    gap = jnp.abs(twice - 2 * other)
    return jnp.where(gap == 0, 1.0, jnp.where(gap == 1, 0.5, 0.0)).astype(F32)


def split(value):
    high = value.astype(BF)
    return high, (value - high.astype(F32)).astype(BF)


def roll(value, shift):
    size = value.shape[-1]
    return value if shift % size == 0 else pltpu.roll(value, shift % size, axis=value.ndim - 1)


def toeplitz_chunks(row):
    block = pltpu.roll(
        jnp.broadcast_to(row, (16, 512)), 1, axis=1, stride=1, stride_axis=0
    )
    block = jnp.concatenate([jnp.zeros((16, 128), F32), block], axis=1)
    return jnp.concatenate([roll(block, -32 * q).astype(BF) for q in range(4)], axis=1)


def place(chunks, index, shift, m):
    q = (-shift) % 4
    n = m + 1 + (-shift - q) // 4
    if 0 <= n <= 4:
        return chunks[index, :, 640 * q + 128 * n : 640 * q + 128 * n + 128]
    return jnp.zeros((16, 128), BF)


def weights(chunks, indices, shifts, lanes):
    return jnp.concatenate(
        [
            jnp.concatenate(
                [place(chunks, i, shift, m) for i in indices for m in range(lanes // 128)],
                axis=1,
            )
            for shift in shifts
        ],
        axis=0,
    )


def terms(s):
    return (1, 2, 3) if isinstance(s, int) and s == 0 else (0, 1, 2, 3)


def each_sum(body, first=0, last=4):
    if first == 0:
        body(0)

    def step(s, _):
        body(s)
        return 0

    lax.fori_loop(max(first, 1), last, step, 0)


def moves(c, size):
    r, l = iota((128, 128), 0), iota((128, 128), 1)
    at = l % size
    ahead = (r == l + c) & (at + c < size)
    behind = ((r == l + c) & (at < size - 4)) | ((r == l + c - size) & (at + c >= size))
    return jnp.concatenate(
        [jnp.where(behind, 1.0, 0.0), jnp.where(ahead, 1.0, 0.0)], axis=1
    ).astype(BF)


def gather(parts, size):
    at = iota(parts[0].shape, 1) % size
    value = parts[2] + jnp.where(at < size - 4, roll(parts[3], -4), 0.0)
    value += jnp.where(at >= 4, roll(parts[1], 4), roll(parts[1], 4 - size))
    back = jnp.where(at >= 4, roll(parts[0], 8 - size), 0.0)
    return value + jnp.where(at >= 8, roll(parts[0], 8), back)


def kernel(
    count_x, count_y,
    charges_in, k_fine, k_mid, k_top, out,
    charges, own, edge, xl, xr, yl, yr, corner,
    mid_pack, mid_edge, mxl, mxr, myl, myr, mid_corner,
    top_pack, top_in,
    taps_in, taps, chunks, inner, outer, acc, mid_acc, top_acc, mid_right, top_right,
    rows_mid, rows_top, zx, pxy, pz,
    load_sem, send_sem, recv_sem,
):
    gx, gy = lax.axis_index("gx"), lax.axis_index("gy")

    def valid(dx, dy):
        ok = jnp.bool_(True)
        if dx:
            ok = (gx + dx >= 0) & (gx + dx < count_x)
        if dy:
            ok = ok & (gy + dy >= 0) & (gy + dy < count_y)
        return ok

    load = pltpu.make_async_copy(charges_in, charges, load_sem)
    load.start()

    @pl.when((gx < 2) | (gx >= count_x - 2) | (gy == 0) | (gy == count_y - 1))
    def _():
        for ref in (yl, yr, corner, mxl, mxr, myl, myr, mid_corner, top_in):
            ref[...] = jnp.zeros_like(ref)

    for ref, dx in ((xl, -1), (xr, 1)):

        @pl.when(~valid(dx, 0))
        def _(ref=ref):
            ref[...] = jnp.zeros_like(ref)

    for ref in (xl.at[0], xr.at[7], mxl.at[0]):
        ref[...] = jnp.zeros(ref.shape, BF)
    barrier = pltpu.get_barrier_semaphore()
    for dx, dy in TOPS:

        @pl.when(valid(dx, dy))
        def _(dx=dx, dy=dy):
            pl.semaphore_signal(
                barrier, inc=1, device_id=(gx + dx, gy + dy), device_id_type=MESH
            )

    taps_in[...] = jnp.zeros_like(taps_in)
    for level, ref in enumerate((k_fine, k_mid, k_top)):
        taps_in[level, :, 0:15, 0:15] = ref[...].astype(F32)
    flat = sum(roll(taps_in[level], 16 * level + 1) for level in range(3))
    flat = flat.reshape(240, 128).astype(BF)
    lane_of = iota((240, 512), 0)
    lane_of = (lane_of // 16) * 32 + lane_of % 16
    spread = jnp.where(lane_of == iota((240, 512), 1), 1.0, 0.0).astype(BF)
    taps[...] = lax.dot_general(
        flat, spread, (((0,), (0,)), ((), ())), preferred_element_type=F32
    )[0:48]

    load.wait()
    own[...] = charges[...].astype(BF)
    edge[0] = charges[:, 0:8, :].reshape(12, 16, 128).astype(BF)
    edge[1] = charges[:, 56:64, :].reshape(12, 16, 128).astype(BF)

    def build(row):
        chunks[row] = toeplitz_chunks(taps[pl.ds(row, 1), :])

    messages = {
        "x_near": (own.at[20:24], xl.at[4:8]),
        "x_far": (own.at[17:20], xl.at[1:4]),
        "x_lo": (own.at[0:7], xr.at[0:7]),
        "y_hi": (edge.at[1], yl),
        "y_lo": (edge.at[0], yr),
        "c_hh": (edge.at[1, 8:12], corner.at[0]),
        "c_hl": (edge.at[0, 8:12], corner.at[1]),
        "c_lh": (edge.at[1, 0:4], corner.at[2]),
        "c_ll": (edge.at[0, 0:4], corner.at[3]),
    }
    copies = {}

    def describe(key, source, target, direction):
        dx, dy = direction
        n = len(copies)
        copies[key] = (
            pltpu.make_async_remote_copy(
                src_ref=source,
                dst_ref=target,
                send_sem=send_sem.at[n],
                recv_sem=recv_sem.at[n],
                device_id=(gx + dx, gy + dy),
                device_id_type=MESH,
            ),
            direction,
        )

    def start(key):
        copy, (dx, dy) = copies[key]

        @pl.when(valid(dx, dy))
        def _():
            copy.start()

    def arrived(key):
        copy, (dx, dy) = copies[key]

        @pl.when(valid(-dx, -dy))
        def _():
            copy.wait_recv()

    def sent(key):
        copy, (dx, dy) = copies[key]

        @pl.when(valid(dx, dy))
        def _():
            copy.wait_send()

    for key, direction in ROUND1:
        describe(key, *messages[key], direction)

    def shift_rows(value, x, target):
        rows = value.shape[0]
        lane = iota((rows, 128), 1)
        for c in range(4):
            turned = roll(value, -c)
            ahead = jnp.where(lane + c < 128, turned, 0.0) if c else turned
            behind = jnp.where((lane < 124) | (lane + c >= 128), turned, 0.0)
            target[1, c, x] = ahead.astype(BF)
            target[0, c, x] = behind.astype(BF)

    def window(side, c, k, t):
        group = pl.ds(8 * k, 8)
        if t == 0:
            parts = [outer[0, side, c, group], inner[side, c, group, 0:16, :]]
        elif t == 3:
            parts = [inner[side, c, group, 32:48, :], outer[1, side, c, group]]
        else:
            parts = [inner[side, c, group, 16 * t - 16 : 16 * t + 16, :]]
        return jnp.concatenate(parts, axis=1).reshape(256, 128)

    def fine_product(s, p, k):
        lo, hi, first = BANDS[k]
        left = weights(
            chunks, [4 * s + c for c in terms(s)], range(first - 14, first - 14 + hi - lo), 256
        )
        right = jnp.concatenate(
            [
                jnp.concatenate([window(s // 2, c, k, t) for t in PAIRS[p]], axis=1)
                for c in terms(s)
            ],
            axis=0,
        )
        return dot(left, right)

    def fine_centre(s, p):
        one, two, three = (fine_product(s, p, k) for k in (1, 2, 3))
        acc[s, p, 0:16] = one[0:16]
        acc[s, p, 16:144] = one[16:144] + two[0:128]
        acc[s, p, 144:240] = one[144:240] + two[128:224] + three[0:96]
        acc[s, p, 240:368] = two[224:352] + three[96:224]
        acc[s, p, 368:384] = three[224:240]

    def first_steps(n, _):
        build(8 + n)
        for h in range(3):
            x = 3 * n + h
            shift_rows(charges[x, 8:56, :], x + 8, inner)
        return 0

    def fine_weights(n, _):
        for h in range(4):
            build(4 * n + h)
        return 0

    lax.fori_loop(0, 2, fine_weights, 0)

    in_x = 1 + jnp.minimum(gx, 2) + jnp.minimum(count_x - 1 - gx, 2)
    in_y = 1 + jnp.minimum(gy, 1) + jnp.minimum(count_y - 1 - gy, 1)
    pl.semaphore_wait(barrier, in_x * in_y - 1)
    for key in EARLY:
        start(key)
    lax.fori_loop(0, 8, first_steps, 0)
    for key in LATE:
        start(key)

    def second_steps(s):
        fine_centre(s, 0)
        for h in range(8):
            build(16 + 8 * s + h)

    each_sum(second_steps, 0, 2)

    r, c = iota((384, 256), 0), iota((384, 256), 1)
    pxy[...] = (near(r // 16, c // 16) * near(r % 16, c % 16)).astype(BF)
    for p in range(2):
        r, c = iota((256, 256), 0), iota((256, 256), 1)
        block = r // 64
        block = jnp.where(block == 1, 2, jnp.where(block == 2, 1, block))
        column_of = jnp.where(c < 128, PAIRS[p][0], PAIRS[p][1])
        pz[p] = jnp.where(block == column_of, near(c % 128, r % 64), 0.0).astype(BF)

    for key in ("x_near", "y_hi", "c_hh"):
        arrived(key)
    r, c = iota((128, 128), 0), iota((128, 128), 1)
    halve = near(r, c % 64).astype(BF)
    quarter = jnp.where(r < 64, near(r, c % 32), 0.0).astype(BF)
    side_rows = yl[...].astype(F32).reshape(24, 8, 128)
    body = jnp.concatenate([side_rows, charges[...]], axis=1).reshape(24 * 72, 128)
    zx[4:28] = dot(body.astype(BF), halve).reshape(24, 72, 128)
    side_rows = corner[0].astype(F32).reshape(8, 8, 128)[4:8]
    body = jnp.concatenate([side_rows, xl[4:8].astype(F32)], axis=1).reshape(4 * 72, 128)
    zx[0:4] = dot(body.astype(BF), halve).reshape(4, 72, 128)
    rows_mid[:, 0:16, :] = jnp.zeros((13, 16, 128), F32)
    for i in range(13):
        rows_mid[i, 16:88, :] = (
            0.5 * zx[2 * i + 1] + zx[2 * i + 2] + 0.5 * zx[2 * i + 3]
        )
    mid = (
        0.5 * rows_mid[:, pl.ds(7, 40, 2), :]
        + rows_mid[:, pl.ds(8, 40, 2), :]
        + 0.5 * rows_mid[:, pl.ds(9, 40, 2), :]
    ).astype(BF)
    mid_rows = mid.astype(F32)
    lane = iota((12, 16, 128), 2)
    packed = jnp.where(lane < 64, mid_rows[1:13, 8:24], mid_rows[1:13, 24:40])
    mid_pack[...] = packed.astype(BF)
    mid_edge[0] = packed[:, 0:8].reshape(6, 16, 128).astype(BF)
    mid_edge[1] = packed[:, 8:16].reshape(6, 16, 128).astype(BF)

    mid_messages = {
        (1, 0): (mid_pack.at[5:12], mxl.at[1:8]),
        (-1, 0): (mid_pack.at[0:8], mxr),
        (0, 1): (mid_edge.at[1], myl),
        (0, -1): (mid_edge.at[0], myr),
        (1, 1): (mid_edge.at[1, 2:6], mid_corner.at[0]),
        (1, -1): (mid_edge.at[0, 2:6], mid_corner.at[1]),
        (-1, 1): (mid_edge.at[1, 0:4], mid_corner.at[2]),
        (-1, -1): (mid_edge.at[0, 0:4], mid_corner.at[3]),
    }
    for direction in MIDS:
        describe(("mid", direction), *mid_messages[direction], direction)
        start(("mid", direction))

    zt = dot(mid_rows.reshape(520, 128).astype(BF), quarter).reshape(13, 40, 128)
    for i in range(6):
        rows_top[i] = 0.5 * zt[2 * i] + zt[2 * i + 1] + 0.5 * zt[2 * i + 2]
    top = (
        0.5 * rows_top[:, pl.ds(7, 16, 2), :]
        + rows_top[:, pl.ds(8, 16, 2), :]
        + 0.5 * rows_top[:, pl.ds(9, 16, 2), :]
    )
    lane = iota((6, 8, 128), 2)
    packed = jnp.where(lane % 64 < 32, top[:, 0:8], top[:, 8:16])
    top_pack[...] = packed.reshape(3, 16, 128).astype(BF)
    for direction in TOPS:
        dx, dy = direction
        part = {2: slice(2, 3), -2: slice(0, 1)}.get(dx, slice(0, 3))
        target = top_in.at[2 - dx, 1 - dy, part]
        describe(("top", direction), top_pack.at[part], target, direction)
        start(("top", direction))

    each_sum(second_steps, 2, 4)

    arrived("y_lo")

    def outer_columns(n, _):
        low, high = yl[n].astype(F32), yr[n].astype(F32)
        for h in range(2):
            x = 2 * n + h
            shift_rows(
                jnp.concatenate([low[8 * h : 8 * h + 8], charges[x, 0:8, :]], axis=0),
                x + 8,
                outer.at[0],
            )
            shift_rows(
                jnp.concatenate([charges[x, 56:64, :], high[8 * h : 8 * h + 8]], axis=0),
                x + 8,
                outer.at[1],
            )
        return 0

    lax.fori_loop(0, 12, outer_columns, 0, unroll=2)

    def third_steps(s):
        fine_centre(s, 1)

    each_sum(third_steps)

    for key in ("x_far", "x_lo", "c_hl", "c_lh", "c_ll"):
        arrived(key)

    def outer_rows(n, _):
        for side, rows in ((0, xl), (1, xr)):
            low = corner[2 * side, n].astype(F32)
            high = corner[2 * side + 1, n].astype(F32)
            for h in range(2):
                x = 2 * n + h
                target = x + 32 * side
                row = rows[x].astype(F32)
                part = slice(8 * h, 8 * h + 8)
                shift_rows(row[8:56], target, inner)
                shift_rows(jnp.concatenate([low[part], row[0:8]], axis=0), target, outer.at[0])
                shift_rows(jnp.concatenate([row[56:64], high[part]], axis=0), target, outer.at[1])
        return 0

    lax.fori_loop(0, 4, outer_rows, 0)

    def fourth_steps(s):
        for p in range(2):
            for k in (0, 4):
                lo, hi, _ = BANDS[k]
                acc[s, p, 16 * lo : 16 * hi, :] += fine_product(s, p, k)

    each_sum(fourth_steps)

    def mid_field(centre, low, high):
        lane = iota(low.shape, 2)
        first = roll(jnp.where(lane < 64, centre[:, 8:16], low), 64)
        last = roll(jnp.where(lane < 64, high, centre[:, 0:8]), 64)
        field = jnp.concatenate([first, centre, last], axis=1)
        return field.reshape(32 * field.shape[0], 128).astype(BF)

    def mid_shift(field, start):
        rows = field.shape[0]
        for c in range(4):
            moved = dot(field, moves(c, 64)).reshape(rows // 32, 32, 256)
            turned = jnp.concatenate([moved[:, 8:32], moved[:, 0:8]], axis=1)
            for side in range(2):
                lanes = slice(128 * side, 128 * side + 128)
                both = jnp.concatenate([moved[:, :, lanes], turned[:, :, lanes]], axis=2)
                mid_right[side, c, start : start + rows, :] = both.reshape(rows, 256).astype(BF)

    def mid_product(s, blocks, start, rows):
        left = weights(
            chunks,
            [16 + 4 * s + c for c in terms(s)],
            [i + 1 - start // 32 for i in blocks],
            rows,
        )
        right = jnp.concatenate(
            [mid_right[s // 2, c, start : start + rows, :] for c in terms(s)], axis=0
        )
        return dot(left, right)

    def pairs(ref):
        value = ref[...].astype(F32)
        return value.reshape(2 * value.shape[0], 8, 128)

    for direction in ((0, 1), (0, -1)):
        arrived(("mid", direction))
    mid_shift(mid_field(mid_pack[...].astype(F32), pairs(myl), pairs(myr)), 256)

    def fifth_steps(s):
        mid_acc[s] = mid_product(s, range(13), 256, 384)

    each_sum(fifth_steps)

    for direction in MIDS:
        if direction[0]:
            arrived(("mid", direction))
    for side, rows in ((0, mxl), (1, mxr)):
        low, high = pairs(mid_corner.at[2 * side]), pairs(mid_corner.at[2 * side + 1])
        mid_shift(mid_field(rows[...].astype(F32), low, high), 640 * side)

    for direction in TOPS:
        arrived(("top", direction))

    def strip(dy):
        parts = []
        for dx in (-2, -1, 0, 1, 2):
            if dx == 0 and dy == 0:
                ref = top_pack
            elif dx == -2:
                ref = top_in.at[0, 1 + dy, 2:3]
            elif dx == 2:
                ref = top_in.at[4, 1 + dy, 0:1]
            else:
                ref = top_in.at[2 + dx, 1 + dy]
            parts.append(pairs(ref))
        return jnp.concatenate(parts, axis=0)

    centre, low, high = strip(0), strip(-1), strip(1)
    lane = iota((22, 8, 128), 2) % 64
    low = roll(jnp.where(lane < 32, centre, low), 32)
    high = roll(jnp.where(lane < 32, high, centre), 32)
    field = jnp.concatenate([low, centre, high], axis=1).reshape(528, 128).astype(BF)
    lane = iota((20, 24, 128), 2)
    for c in range(4):
        moved = dot(field, moves(c, 32)).reshape(22, 24, 256)
        moved = jnp.concatenate([moved, jnp.zeros((2, 24, 256), F32)], axis=0)
        for side in range(2):
            part = moved[:, :, 128 * side : 128 * side + 128]
            both = jnp.where(lane < 64, part[0:20], part[4:24])
            both = jnp.concatenate([both, jnp.zeros((20, 8, 128), F32)], axis=1)
            top_right[side, c] = both.reshape(640, 128).astype(BF)

    def sixth_steps(s):
        mid_acc[s, 0:112, :] += mid_product(s, range(7), 0, 256)
        mid_acc[s, 80:208, :] += mid_product(s, range(5, 13), 640, 256)
        left = weights(chunks, [32 + 4 * s + c for c in terms(s)], range(1, 5), 640)
        right = jnp.concatenate([top_right[s // 2, c] for c in terms(s)], axis=0)
        top_acc[s] = dot(left, right)

    each_sum(sixth_steps)

    last_x, last_y = gx == count_x - 1, gy == count_y - 1
    r, c = iota((128, 128), 0), iota((128, 128), 1)
    beyond = (last_x & (r // 16 == 6)) | (last_y & (r % 16 == 8) & (c % 64 >= 32))
    top_e = gather([top_acc[s] for s in range(4)], 32)
    top_e = jnp.concatenate([top_e, roll(top_e, 64)], axis=0)
    high, low = split(jnp.where(beyond, 0.0, top_e))
    stretch = jnp.where(
        (r < 64) & (r // 32 == c // 64), near(c % 64, r % 32), 0.0
    ).astype(BF)
    wide = dot(
        jnp.concatenate([high, low], axis=1), jnp.concatenate([stretch, stretch], axis=0)
    )
    wide = jnp.concatenate(split(wide), axis=0)
    r, c = iota((208, 128), 0), iota((208, 128), 1)
    along_x = near(r // 16, c // 16)
    parts = []
    for parity in range(2):
        spread = (along_x * near(8 * parity + r % 16, c % 16)).astype(BF)
        parts.append(dot(jnp.concatenate([spread, spread], axis=1), wide))
    mid_u = gather([mid_acc[s] for s in range(4)], 64) + jnp.concatenate(parts, axis=1)

    r, c = iota((208, 256), 0), iota((208, 256), 1)
    beyond = (last_x & (r // 16 == 12)) | (last_y & (r % 16 == 8) & (c >= 192))
    mid_u = jnp.concatenate(split(jnp.where(beyond, 0.0, mid_u)), axis=1)
    spread = jnp.concatenate([pxy[...], pxy[...]], axis=1)
    lane = iota((384, 128), 1)
    for p in range(2):
        wide = dot(mid_u, jnp.concatenate([pz[p], pz[p]], axis=0))
        high, low = split(jnp.concatenate([wide, jnp.zeros((48, 256), F32)], axis=0))
        total = dot(spread, jnp.concatenate([high, low], axis=0))
        for h in range(2):
            lanes = slice(128 * h, 128 * h + 128)
            value = total[:, lanes] + acc[2, p, :, lanes]
            value += jnp.where(lane < 124, roll(acc[3, p, :, lanes], -4), 0.0)
            value += roll(acc[1, p, :, lanes], 4)
            value += jnp.where(lane >= 4, roll(acc[0, p, :, lanes], 8), 0.0)
            t = PAIRS[p][h]
            out[:, 16 * t : 16 * t + 16, :] = value.reshape(24, 16, 128)

    for key in copies:
        sent(key)


def solution(mesh):
    count_x, count_y = mesh.shape["gx"], mesh.shape["gy"]
    vmem = pl.BlockSpec(memory_space=pltpu.VMEM)
    messages = len(ROUND1) + len(MIDS) + len(TOPS)

    def shards(charges, kernel_fine, kernel_mid, kernel_top):
        return pl.pallas_call(
            functools.partial(kernel, count_x, count_y),
            out_shape=pltpu.VMEM(charges.shape, F32),
            in_specs=[pl.BlockSpec(memory_space=pl.ANY)] + [vmem] * 3,
            out_specs=vmem,
            scratch_shapes=[
                pltpu.VMEM((24, 64, 128), F32),
                pltpu.VMEM((24, 64, 128), BF),
                pltpu.VMEM((2, 12, 16, 128), BF),
                pltpu.VMEM((8, 64, 128), BF),
                pltpu.VMEM((8, 64, 128), BF),
                pltpu.VMEM((12, 16, 128), BF),
                pltpu.VMEM((12, 16, 128), BF),
                pltpu.VMEM((4, 4, 16, 128), BF),
                pltpu.VMEM((12, 16, 128), BF),
                pltpu.VMEM((2, 6, 16, 128), BF),
                pltpu.VMEM((8, 16, 128), BF),
                pltpu.VMEM((8, 16, 128), BF),
                pltpu.VMEM((6, 16, 128), BF),
                pltpu.VMEM((6, 16, 128), BF),
                pltpu.VMEM((4, 4, 16, 128), BF),
                pltpu.VMEM((3, 16, 128), BF),
                pltpu.VMEM((5, 3, 3, 16, 128), BF),
                pltpu.VMEM((3, 15, 16, 128), F32),
                pltpu.VMEM((48, 512), F32),
                pltpu.VMEM((48, 16, 2560), BF),
                pltpu.VMEM((2, 4, 40, 48, 128), BF),
                pltpu.VMEM((2, 2, 4, 40, 16, 128), BF),
                pltpu.VMEM((4, 2, 384, 256), F32),
                pltpu.VMEM((4, 208, 256), F32),
                pltpu.VMEM((4, 64, 128), F32),
                pltpu.VMEM((2, 4, 896, 256), BF),
                pltpu.VMEM((2, 4, 640, 128), BF),
                pltpu.VMEM((13, 88, 128), F32),
                pltpu.VMEM((6, 40, 128), F32),
                pltpu.VMEM((28, 72, 128), F32),
                pltpu.VMEM((384, 256), BF),
                pltpu.VMEM((2, 256, 256), BF),
                pltpu.SemaphoreType.DMA,
                pltpu.SemaphoreType.DMA((messages,)),
                pltpu.SemaphoreType.DMA((messages,)),
            ],
            compiler_params=pltpu.CompilerParams(
                collective_id=0, has_side_effects=True, vmem_limit_bytes=56 * 2**20
            ),
        )(charges, kernel_fine, kernel_mid, kernel_top)

    placed = (P("gx", "gy", None), P(), P(), P())
    return jax.shard_map(
        shards, mesh=mesh, in_specs=placed, out_specs=P("gx", "gy", None), check_vma=False
    )
```
